256 devices in a mesh: dp: 128 (over y, x_lo, z, core), pair: 2 (over x_hi).
Axes of the slice: x: 4 (x_hi: 2, x_lo: 2; x = x_hi * 2 + x_lo), y: 4, z: 8, core: 2. Of those that a mesh axis runs over, the one named last changes fastest.
Arguments:
- queries: bfloat16 [2048, 4096], P('dp', 'pair'), may hold values from -6 to 6
- passages: bfloat16 [2048, 4096], P('dp', 'pair'), may hold values from -6 to 6
- hard_passages: bfloat16 [2048, 4096], P('dp', 'pair'), may hold values from -6 to 6
- positive_ids: int32 [2048], P('dp'), may hold values from 0 to 2047, each once
- hard_ids: int32 [2048, 8], P('dp'), may hold values from 0 to 2047, as said below
Outputs:
- mean_loss: float32 [1], replicated
- grad_queries: bfloat16 [2048, 4096], P('dp', 'pair')
- grad_passages: bfloat16 [2048, 4096], P('dp', 'pair')
- grad_hard: bfloat16 [2048, 4096], P('dp', 'pair')
The draws below stay inside these ranges and needn't reach their ends.
Inputs may be any that keep to these rules, and one draw needn't show every extreme that they name: A permutation: query i's positive passage is positive_ids[i]. `hard_ids`: of the 128 ids held with the queries of one index of dp, at most 2 fall in the pool rows of any one index r of dp (rows r * 16 to (r + 1) * 16 - 1). Ids may repeat.
All inputs are finite; a program needn't handle non-finite values.
Results may differ from the reference program's by a relative error of at most 0.0049.
Values may be sent and summed in bfloat16 or wider, within the bound.
No kernel may reach another device: no remote copies, remote signals or barrier semaphores. Data moves between devices by JAX's collectives and lax.ppermute only.
A program may use at most 128 MiB of HBM per device.

```python
import math
import jax
import jax.numpy as jnp
from jax import lax

D = 4096
Q_DEV = 16
K_HARD = 8
BATCH = 2048
HARD_POOL = 2048
CAP = 2


def draw_hard_ids(key, part):
    key = jax.random.fold_in(key, 11)
    num_devices = HARD_POOL // Q_DEV
    entries = Q_DEV * K_HARD
    total_slots = num_devices * CAP
    keys = jax.random.split(key, 6)
    hot_global = jax.random.randint(keys[0], (), 0, num_devices)
    hot_local = jax.random.randint(keys[1], (num_devices,), 0, num_devices)
    favoured = jax.random.randint(keys[2], (num_devices,), 0, 2)
    slot_owner = jnp.arange(total_slots, dtype=jnp.int32) // CAP
    noise = jax.random.randint(keys[3], (num_devices, total_slots), 0, 4096)
    tier = favoured[slot_owner][None, :]
    tier = tier + 4 * (slot_owner[None, :] == hot_local[:, None]).astype(jnp.int32)
    tier = tier + 8 * (slot_owner[None, :] == hot_global).astype(jnp.int32)
    ranking = (tier * 4096 + noise) * total_slots + jnp.arange(total_slots, dtype=jnp.int32)[None, :]
    top_values, chosen = lax.top_k(ranking, entries)
    owners = chosen // CAP
    perms = jax.vmap(lambda sub_key: jax.random.permutation(sub_key, entries))(jax.random.split(keys[4], num_devices))
    owners = jnp.take_along_axis(owners, perms, axis=1)
    offsets = jax.random.randint(keys[5], (num_devices, entries), 0, Q_DEV)
    return (owners * Q_DEV + offsets).reshape(BATCH, K_HARD).astype(jnp.int32)


def steps_of(rng, dims, shards, smallest, largest):
    gain, own = 1.0, jax.random.fold_in(rng, 6)
    for axis_at, parts in shards:
        heights = jnp.exp(jax.random.uniform(jax.random.fold_in(own, axis_at), (parts,), jnp.float32, smallest / len(shards), largest / len(shards)))
        gain = gain * jnp.repeat(heights, dims[axis_at] // parts).reshape([-1 if axis == axis_at else 1 for axis in range(len(dims))])
    return gain


def gaussian(key, extent, width, bound, pieces=(), kind=jnp.bfloat16):
    loudness = steps_of(key, extent, pieces, -0.22, 0.18) if pieces else 1.0
    values = jax.random.normal(key, extent, jnp.float32) * width * loudness
    return jnp.minimum(jnp.maximum(values, -bound), bound).astype(kind)


def setup_inputs(seed: int = 0) -> dict:
    seeds = jax.random.split(jax.random.key(seed), 6)
    return {
        "queries": gaussian(seeds[0], (BATCH, D), 1.0, 6.0, ((0, 128), (1, 2))),
        "passages": gaussian(seeds[1], (BATCH, D), 1.0, 6.0, ((0, 128), (1, 2))),
        "hard_passages": gaussian(seeds[2], (HARD_POOL, D), 1.0, 6.0, ((0, 128), (1, 2))),
        "positive_ids": jax.random.permutation(seeds[3], BATCH).astype(jnp.int32),
        "hard_ids": draw_hard_ids(jax.random.fold_in(seeds[5], 71), 0),
    }


logit_bias = -1.0

def reference(queries, passages, hard_passages, positive_ids, hard_ids):
    scale_factor = 1.0 / math.sqrt(D)
    scores = jnp.dot(queries, passages.T, preferred_element_type=jnp.float32)
    columns = jnp.arange(BATCH, dtype=jnp.int32)
    labels = (columns[None, :] == positive_ids[:, None]).astype(jnp.float32)
    logits = scale_factor * scores + logit_bias
    weights = ((jax.nn.sigmoid(logits) - labels) * scale_factor).astype(jnp.bfloat16)
    hard_rows = jnp.take(hard_passages, hard_ids.reshape(-1), axis=0).reshape(BATCH, K_HARD, D)
    hard_scores = jnp.einsum('qkd,qd->qk', hard_rows.astype(jnp.float32), queries.astype(jnp.float32), precision=lax.Precision.HIGHEST)
    hard_logits = scale_factor * hard_scores + logit_bias
    hard_weights = (jax.nn.sigmoid(hard_logits) * scale_factor).astype(jnp.bfloat16)
    total = jnp.sum(jax.nn.softplus(logits) - labels * logits) + jnp.sum(jax.nn.softplus(hard_logits))
    mean_loss = (total / (BATCH * (BATCH + K_HARD))).reshape(1)
    pool_cols = jnp.arange(HARD_POOL, dtype=jnp.int32)
    hard_dense = lax.optimization_barrier(jnp.sum((hard_ids[:, :, None] == pool_cols[None, None, :]).astype(jnp.float32) * hard_weights.astype(jnp.float32)[:, :, None], axis=1))
    grad_queries = jnp.dot(weights.astype(jnp.float32), passages.astype(jnp.float32), precision=lax.Precision.HIGHEST)
    grad_queries = grad_queries + jnp.dot(hard_dense, hard_passages.astype(jnp.float32), precision=lax.Precision.HIGHEST)
    grad_passages = jnp.dot(weights.astype(jnp.float32).T, queries.astype(jnp.float32), precision=lax.Precision.HIGHEST)
    grad_hard = jnp.dot(hard_dense.T, queries.astype(jnp.float32), precision=lax.Precision.HIGHEST)
    return (mean_loss, grad_queries.astype(jnp.bfloat16), grad_passages.astype(jnp.bfloat16), grad_hard.astype(jnp.bfloat16))
```

```python
import math

import jax
import jax.numpy as jnp
from jax import lax
from jax.experimental import pallas as pl
from jax.experimental.pallas import tpu as pltpu
from jax.sharding import Mesh, PartitionSpec as P

D = 4096
SCALE = 1.0 / math.sqrt(D)
LOGIT_BIAS = -1.0
BF16, F32 = jnp.bfloat16, jnp.float32

SHAPE = (4, 2, 8, 2, 2)
DP = ("y", "xl", "z", "core")
PLANE = ("y", "xl")
LINE = ("z", "core")
NY, NX, NZ = 4, 2, 8
STEPS = [(dy, dx) for dy in range(NY) for dx in range(NX)]


def call(kernel, outs, *args, flops=0):
    shapes = [jax.ShapeDtypeStruct(s, t) for s, t in outs]
    size = sum(math.prod(s) * jnp.dtype(t).itemsize for s, t in outs) + sum(a.size * a.dtype.itemsize for a in args)
    return pl.pallas_call(
        kernel,
        out_shape=shapes,
        compiler_params=pltpu.CompilerParams(vmem_limit_bytes=24 << 20),
        cost_estimate=pl.CostEstimate(flops=flops, bytes_accessed=size, transcendentals=0),
    )(*args)


def call_scratch(kernel, outs, scratch, *args, flops=0):
    shapes = [jax.ShapeDtypeStruct(s, t) for s, t in outs]
    size = sum(math.prod(s) * jnp.dtype(t).itemsize for s, t in outs) + sum(a.size * a.dtype.itemsize for a in args)
    return pl.pallas_call(
        kernel,
        out_shape=shapes,
        scratch_shapes=[pltpu.VMEM(s, t) for s, t in scratch],
        compiler_params=pltpu.CompilerParams(vmem_limit_bytes=24 << 20),
        cost_estimate=pl.CostEstimate(flops=flops, bytes_accessed=size, transcendentals=0),
    )(*args)


def from_plane(x, step):
    dy, dx = step
    pairs = []
    for y in range(NY):
        for xl in range(NX):
            pairs.append((((y + dy) % NY) * NX + (xl + dx) % NX, y * NX + xl))
    return lax.ppermute(x, PLANE, pairs)


def from_line(x, step, back=False):
    pairs = []
    for z in range(NZ):
        for core in range(2):
            way = step if (core == 0) != back else -step
            pairs.append((((z + way) % NZ) * 2 + core, z * 2 + core))
    return lax.ppermute(x, LINE, pairs)


def from_core(x):
    return lax.ppermute(x, "core", [(0, 1), (1, 0)])


def scores_kernel(*refs):
    q_refs, p_refs, (s_ref, ids_ref, q_all, p_all) = refs[:9], refs[9:17], refs[17:]
    width = p_all.shape[1]
    at = 0
    for ref in q_refs:
        n = ref.shape[0]
        q_all[at : at + n, :] = ref[:, :width]
        ids_ref[at : at + n, :] = ref[:, width:]
        at += n
    at = 0
    for ref in p_refs:
        n = ref.shape[0]
        p_all[at : at + n, :] = ref[...]
        at += n
    s_ref[...] = lax.dot_general(q_all[...], p_all[...], (((1,), (1,)), ((), ())), preferred_element_type=F32)


def weights_kernel(s_ref, got_ref, ids_ref, cols_ref, hard_ref, w_ref, loss_ref):
    logits = SCALE * (s_ref[...] + got_ref[...]) + LOGIT_BIAS
    col = jnp.broadcast_to(cols_ref[...], logits.shape)
    hard = jnp.broadcast_to(hard_ref[...], logits.shape) > 0.0
    ids = ids_ref[...].astype(F32)

    def hits(k):
        return (ids[:, 2 * k : 2 * k + 1] * 16.0 + ids[:, 2 * k + 1 : 2 * k + 2] == col).astype(F32)

    labels = hits(0)
    counts = hits(1)
    for k in range(2, 9):
        counts = counts + hits(k)
    e = jnp.exp(-jnp.abs(logits))
    sigmoid = jnp.where(logits >= 0.0, 1.0, e) / (1.0 + e)
    softplus = jnp.maximum(logits, 0.0) + jnp.log1p(e)
    in_batch = ((sigmoid - labels) * SCALE).astype(BF16)
    picked = (counts * (sigmoid * SCALE).astype(BF16).astype(F32)).astype(BF16)
    w_ref[...] = jnp.where(hard, picked, in_batch)
    loss = jnp.sum(jnp.where(hard, counts * softplus, softplus - labels * logits))
    loss_ref[...] = jnp.full(loss_ref.shape, loss, F32)


def grad_q_kernel(w_ref, *refs):
    p_refs, (keep_ref, send_ref, p_all) = refs[:8], refs[8:]
    at = 0
    for ref in p_refs:
        n = ref.shape[0]
        p_all[at : at + n, :] = ref[...]
        at += n
    part = jnp.dot(w_ref[...], p_all[...], preferred_element_type=F32)
    keep_ref[...] = part[:144, :]
    send_ref[...] = part[144:, :].astype(BF16)


def grad_p_kernel(w_ref, *refs):
    q_refs, p_outs, q_all = refs[:9], refs[9:17], refs[17]
    width = q_all.shape[1]
    at = 0
    for ref in q_refs:
        n = ref.shape[0]
        q_all[at : at + n, :] = ref[:, :width]
        at += n
    part = lax.dot_general(w_ref[...], q_all[...], (((0,), (0,)), ((), ())), preferred_element_type=F32)
    for k, ref in enumerate(p_outs):
        ref[...] = part[32 * k : 32 * k + 32, :].astype(ref.dtype)


def join_kernel(keep_ref, got_ref, *out_refs):
    at = 0
    for ref in out_refs:
        n = ref.shape[0]
        ref[...] = (keep_ref[32 + at : 32 + at + n, :] + got_ref[at : at + n, :].astype(F32)).astype(BF16)
        at += n


def solution(mesh):
    fine = Mesh(mesh.devices.reshape(SHAPE), DP + ("pair",))

    def on_device(queries, passages, hard_passages, positive_ids, hard_ids):
        rows, width = queries.shape
        batch = rows * NY * NX * NZ * 2
        per_query = hard_ids.shape[1]
        core = lax.axis_index("core")

        ids = jnp.concatenate([positive_ids[:, None], hard_ids], axis=1)
        ids = jnp.stack([ids // 16, ids % 16], axis=2).reshape(rows, 18)
        ids = jnp.pad(ids, ((0, 0), (0, 110))).astype(BF16)
        own_q = jnp.concatenate([queries, ids], axis=1)
        chip_q = lax.all_gather(own_q, "core", axis=0, tiled=True)
        own_p = jnp.concatenate([passages, hard_passages], axis=0)

        near_q = [from_line(chip_q, step) for step in (1, 2, 3)] + [from_line(own_q, 4)]
        block_p = [own_p] + [from_plane(own_p, step) for step in STEPS[1:]]
        far_q = [from_core(x) for x in near_q]
        block_q = [chip_q] + near_q + far_q

        place = jnp.arange(32, dtype=jnp.int32)
        owners = []
        for dy, dx in STEPS:
            y = (lax.axis_index("y") + dy) % NY
            x = (lax.axis_index("xl") + dx) % NX
            owners.append((y * NX + x) * (NZ * 2) + lax.axis_index(LINE))
        owners = jnp.stack(owners)
        cols = (owners[:, None] * rows + place[None, :] % rows).reshape(1, 256).astype(F32)
        hard = jnp.broadcast_to(place[None, :] >= rows, (8, 32)).reshape(1, 256).astype(F32)

        scores, ids_all = call_scratch(
            scores_kernel,
            [((256, 256), F32), ((256, 128), BF16)],
            [((256, width), BF16), ((256, width), BF16)],
            *block_q,
            *block_p,
        )
        other = lax.ppermute(scores, "pair", [(0, 1), (1, 0)])
        weights, loss = call(
            weights_kernel, [((256, 256), BF16), ((8, 128), F32)], scores, other, ids_all, cols, hard
        )

        loss = loss + from_core(loss)
        for step in (4, 2, 1):
            loss = loss + from_line(loss, step)
        for step in ((2, 0), (1, 0), (0, 1)):
            loss = loss + from_plane(loss, step)
        mean_loss = loss[0, :1] / (batch * (batch + per_query))

        keep, send = call_scratch(
            grad_q_kernel, [((144, width), F32), ((112, width), BF16)], [((256, width), BF16)], weights, *block_p
        )
        got = from_core(send)
        outs = call_scratch(
            grad_p_kernel,
            [((32, width), F32)] + [((32, width), BF16)] * 7,
            [((256, width), BF16)],
            weights,
            *block_q,
        )
        total_p = outs[0]
        for part, (dy, dx) in zip(outs[1:], STEPS[1:]):
            total_p = total_p + from_plane(part, (-dy, -dx)).astype(F32)

        parts = call(join_kernel, [((32, width), BF16)] * 3 + [((16, width), BF16)], keep, got)
        back = [from_line(x, step, back=True) for x, step in zip(parts, (1, 2, 3, 4))]
        chip = keep[:32] + back[0].astype(F32) + back[1].astype(F32) + back[2].astype(F32)
        mine = lax.dynamic_slice_in_dim(chip, core * rows, rows, 0) + back[3].astype(F32)
        theirs = lax.dynamic_slice_in_dim(chip, (1 - core) * rows, rows, 0)
        grad_q = mine + from_core(theirs)
        return (
            mean_loss,
            grad_q.astype(BF16),
            total_p[:rows].astype(BF16),
            total_p[rows:].astype(BF16),
        )

    wide = P(DP, "pair")
    return jax.shard_map(
        on_device,
        mesh=fine,
        in_specs=(wide, wide, wide, P(DP), P(DP, None)),
        out_specs=(P(), wide, wide, wide),
        check_vma=False,
    )
```

```python
import math

import jax
import jax.numpy as jnp
from jax import lax
from jax.experimental import pallas as pl
from jax.experimental.pallas import tpu as pltpu
from jax.sharding import Mesh, PartitionSpec as P

D = 4096
SCALE = 1.0 / math.sqrt(D)
LOGIT_BIAS = -1.0
BF16, F32, I32 = jnp.bfloat16, jnp.float32, jnp.int32

SHAPE = (4, 2, 8, 2, 2)
DP = ("y", "xl", "z", "core")
PLANE = ("y", "xl")
LINE = ("z", "core")
NY, NX, NZ = 4, 2, 8
STEPS = [(dy, dx) for dy in range(NY) for dx in range(NX)]


def call(kernel, outs, *args, scratch=(), after=()):
    count = len(args)

    def body(*refs):
        kernel(*refs[:count], *refs[count + len(after) :])

    return pl.pallas_call(
        body,
        out_shape=[jax.ShapeDtypeStruct(s, t) for s, t in outs],
        in_specs=[pl.BlockSpec(memory_space=pltpu.VMEM)] * count + [pl.BlockSpec(memory_space=pl.ANY)] * len(after),
        out_specs=[pl.BlockSpec(memory_space=pltpu.VMEM) for _ in outs],
        scratch_shapes=[pltpu.VMEM(s, t) for s, t in scratch],
        compiler_params=pltpu.CompilerParams(vmem_limit_bytes=12 << 20),
    )(*args, *after)


def from_plane(x, step):
    dy, dx = step
    pairs = []
    for y in range(NY):
        for xl in range(NX):
            pairs.append((((y + dy) % NY) * NX + (xl + dx) % NX, y * NX + xl))
    return lax.ppermute(x, PLANE, pairs)


def from_line(x, step, back=False):
    pairs = []
    for z in range(NZ):
        for core in range(2):
            way = step if (core == 0) != back else -step
            pairs.append((((z + way) % NZ) * 2 + core, z * 2 + core))
    return lax.ppermute(x, LINE, pairs)


def from_core(x):
    return lax.ppermute(x, "core", [(0, 1), (1, 0)])


def pack(refs, scratch):
    at, width = 0, scratch.shape[1]
    for ref in refs:
        n = ref.shape[0]
        scratch[at : at + n, :] = ref[:, :width]
        at += n


def lanes3(x, first, shape):
    lane = lax.broadcasted_iota(I32, shape, 1)
    high = x.astype(BF16).astype(F32)
    mid = (x - high).astype(BF16).astype(F32)
    low = (x - high - mid).astype(BF16).astype(F32)
    out = jnp.zeros(shape, F32)
    for i, part in enumerate((high, mid, low)):
        out = jnp.where(lane == first + i, jnp.broadcast_to(part, shape), out)
    return out


def sum_lanes(x, first):
    lane = lax.broadcasted_iota(I32, (1, 128), 1)
    return jnp.sum(jnp.where((lane >= first) & (lane < first + 3), x[:1, :].astype(F32), 0.0), axis=1, keepdims=True)


def own_kernel(q_ref, p_ref, h_ref, pos_ref, hard_ref, own_q, own_p):
    rows, width = q_ref.shape
    own_q[:, :width] = q_ref[...]
    own_p[:rows, :] = p_ref[...]
    own_p[rows:, :] = h_ref[...]
    lane = lax.broadcasted_iota(I32, (8, 128), 1)
    row = lax.broadcasted_iota(I32, (8, 128), 0)
    ids = jnp.zeros((rows, 128), F32)
    first = jnp.broadcast_to(pos_ref[...], (8, rows))
    for shift, part in ((0, lambda v: v // 16), (16, lambda v: v % 16)):
        at = jnp.where(lane == row + 1 + shift, 1.0, 0.0).astype(BF16)
        ids = ids + jnp.dot(part(hard_ref[...]).astype(F32).astype(BF16), at, preferred_element_type=F32)
        at = jnp.where((lane == shift) & (row == 0), 1.0, 0.0).astype(BF16)
        ids = ids + lax.dot_general(
            part(first).astype(F32).astype(BF16), at, (((0,), (0,)), ((), ())), preferred_element_type=F32
        )
    own_q[:, width:] = ids.astype(BF16)


def both_kernel(own_p, other_p, other_h, own_q, other_q, row_p, chip_q):
    pack((own_p, other_p, other_h), row_p)
    pack((own_q, other_q), chip_q)


def pack_kernel(*refs):
    pack(refs[:-1], refs[-1])


def far_kernel(near1, near2, far, both):
    far[:32, :] = near1[...]
    far[32:, :] = near2[:16, :]
    pack((near1, near2), both)


def scores_kernel(*refs):
    q_refs, p_refs, (s_ref, ids_ref, q_all, p_all) = refs[:3], refs[3:7], refs[7:]
    width = p_all.shape[1]
    pack(q_refs, q_all)
    pack(p_refs, p_all)
    at = 0
    for ref in q_refs:
        n = ref.shape[0]
        ids_ref[at : at + n, :] = ref[:, width:]
        at += n
    s_ref[...] = lax.dot_general(q_all[...], p_all[...], (((1,), (1,)), ((), ())), preferred_element_type=F32)


def weights_kernel(s_ref, got_ref, ids_ref, cols_ref, hard_ref, w_ref, loss_ref):
    logits = SCALE * (s_ref[...] + got_ref[...]) + LOGIT_BIAS
    col = jnp.broadcast_to(cols_ref[...], logits.shape)
    hard = jnp.broadcast_to(hard_ref[...], logits.shape) > 0.0
    ids = ids_ref[...].astype(F32)

    def hits(k):
        return (ids[:, k : k + 1] * 16.0 + ids[:, 16 + k : 17 + k] == col).astype(F32)

    labels = hits(0)
    counts = hits(1)
    for k in range(2, 9):
        counts = counts + hits(k)
    e = jnp.exp(-jnp.abs(logits))
    sigmoid = jnp.where(logits >= 0.0, 1.0, e) / (1.0 + e)
    softplus = jnp.maximum(logits, 0.0) + jnp.log1p(e)
    in_batch = ((sigmoid - labels) * SCALE).astype(BF16)
    picked = (counts * (sigmoid * SCALE).astype(BF16).astype(F32)).astype(BF16)
    w_ref[...] = jnp.where(hard, picked, in_batch)
    loss = jnp.sum(jnp.where(hard, counts * softplus, softplus - labels * logits), axis=1, keepdims=True)
    loss = jnp.sum(loss, axis=0, keepdims=True)
    loss_ref[...] = jnp.broadcast_to(loss, loss_ref.shape)


def grad_q_kernel(w_ref, loss_ref, *refs):
    p_refs, (keep_ref, send_ref, p_all) = refs[:4], refs[4:]
    pack(p_refs, p_all)
    part = jnp.dot(w_ref[...], p_all[...], preferred_element_type=F32)
    keep_ref[...] = part[:144, :]
    send_ref[:112, :] = part[144:, :].astype(BF16)
    send_ref[112:, :128] = lanes3(loss_ref[:1, :1], 0, (16, 128)).astype(BF16)
    send_ref[112:, 128:] = jnp.zeros((16, send_ref.shape[1] - 128), BF16)


def grad_p_kernel(steps):
    def kernel(w_ref, *refs):
        q_refs, p_outs, q_all = refs[:3], refs[3:-1], refs[-1]
        pack(q_refs, q_all)
        for step, ref in zip(steps, p_outs):
            w = w_ref[...][:, 64 * step : 64 * step + 64]
            part = lax.dot_general(w, q_all[...], (((0,), (0,)), ((), ())), preferred_element_type=F32)
            ref[...] = part.astype(ref.dtype)

    return kernel


def far_sum_kernel(keep_ref, got_ref, loss_ref, far_ref, chip_loss_ref):
    width = keep_ref.shape[1]
    loss = loss_ref[:1, :1] + sum_lanes(got_ref[112:, :128], 0)
    chip_loss_ref[...] = jnp.broadcast_to(loss, chip_loss_ref.shape)
    far_ref[:, :width] = (keep_ref[96:144, :] + got_ref[64:112, :].astype(F32)).astype(BF16)
    far_ref[:, width:] = lanes3(loss, 0, (48, 128)).astype(BF16)


def near_sum_kernel(keep_ref, got_ref, far_ref, loss_ref, near1_ref, near2_ref):
    width = keep_ref.shape[1]
    far_loss = sum_lanes(far_ref[:16, width:], 0)
    lanes = (lanes3(loss_ref[:1, :1], 0, (32, 128)) + lanes3(far_loss, 3, (32, 128))).astype(BF16)
    near1_ref[:, width:] = lanes
    near2_ref[:, width:] = lanes
    near1 = keep_ref[32:64, :] + got_ref[:32, :].astype(F32) + far_ref[:32, :width].astype(F32)
    near1_ref[:, :width] = near1.astype(BF16)
    near2 = keep_ref[64:80, :] + got_ref[32:48, :].astype(F32) + far_ref[32:, :width].astype(F32)
    near2_ref[:16, :width] = near2.astype(BF16)
    near2_ref[16:, :width] = (keep_ref[80:96, :] + got_ref[48:64, :].astype(F32)).astype(BF16)


def chip_sum_kernel(keep_ref, b1, b2, loss_ref, rel_ref, mine_ref, theirs_ref, line_ref):
    rows, width = mine_ref.shape
    rel = rel_ref[...]
    line = jnp.where(rel == 0, loss_ref[:1, :1], 0.0)
    for step, ref, first in ((1, b1, 0), (3, b1, 3), (2, b2, 0), (4, b2, 3)):
        line = jnp.where(rel == step, sum_lanes(ref[:16, width:], first), line)
    line_ref[...] = jnp.broadcast_to(line[None], line_ref.shape)
    total = keep_ref[: 2 * rows, :] + b1[:, :width].astype(F32) + b2[:, :width].astype(F32)
    mine_ref[...] = total[:rows, :]
    theirs_ref[...] = total[rows:, :]


def finish_q_kernel(mine_ref, got_ref, out_ref):
    out_ref[...] = (mine_ref[...] + got_ref[...]).astype(BF16)


def row_sum_kernel(own_ref, b1, b2, b3, mine_ref, theirs_ref):
    total = own_ref[...]
    for ref in (b1, b2, b3):
        total = total + ref[...].astype(F32)
    mine_ref[...] = total[:32, :]
    theirs_ref[...] = total[32:, :].astype(BF16)


def finish_p_kernel(mine_ref, got_ref, p_ref, h_ref):
    rows = p_ref.shape[0]
    total = mine_ref[...] + got_ref[...].astype(F32)
    p_ref[...] = total[:rows, :].astype(BF16)
    h_ref[...] = total[rows:, :].astype(BF16)


def on_device(queries, passages, hard_passages, positive_ids, hard_ids):
    rows, width = queries.shape
    wide = width + 128
    batch = rows * NY * NX * NZ * 2
    per_query = hard_ids.shape[1]
    core, z = lax.axis_index("core"), lax.axis_index("z")

    other_p, other_h = from_plane(passages, (0, 1)), from_plane(hard_passages, (0, 1))
    own_q, own_p = call(
        own_kernel,
        [((rows, wide), BF16), ((2 * rows, width), BF16)],
        queries,
        passages,
        hard_passages,
        positive_ids.reshape(1, rows),
        hard_ids,
    )
    row_p, chip_q = call(
        both_kernel,
        [((4 * rows, width), BF16), ((2 * rows, wide), BF16)],
        own_p,
        other_p,
        other_h,
        own_q,
        from_core(own_q),
    )
    near1, near2 = from_line(chip_q, 1), from_line(chip_q, 2)
    block_p = [row_p] + [from_plane(row_p, (dy, 0)) for dy in (1, 2, 3)]
    far, both = call(
        far_kernel, [((48, wide), BF16), ((64, wide), BF16)], near1, near2, after=[block_p[1], block_p[3]]
    )
    far = from_line(far, 2)
    (near,) = call(pack_kernel, [((144, wide), BF16)], chip_q, near1, near2, far)
    block_q = [near, from_core(both), from_core(far)]

    place = jnp.arange(32, dtype=I32)
    owners = []
    for dy, dx in STEPS:
        y = (lax.axis_index("y") + dy) % NY
        x = (lax.axis_index("xl") + dx) % NX
        owners.append((y * NX + x) * (NZ * 2) + lax.axis_index(LINE))
    owners = jnp.stack(owners)
    cols = (owners[:, None] * rows + place[None, :] % rows).reshape(1, 256).astype(F32)
    hard = jnp.broadcast_to(place[None, :] >= rows, (8, 32)).reshape(1, 256).astype(F32)
    lane = jnp.arange(128, dtype=I32)[None, :]
    rel = jnp.where(lane < NZ, jnp.where(core == 0, z - lane, lane - z) % NZ, NZ)
    rel = jnp.where((core == 1) & (rel % 4 == 0), NZ, rel)

    scores, ids_all = call(
        scores_kernel,
        [((256, 256), F32), ((256, 128), BF16)],
        *block_q,
        *block_p,
        scratch=[((256, width), BF16), ((256, width), BF16)],
    )
    other = lax.ppermute(scores, "pair", [(0, 1), (1, 0)])
    weights, loss = call(
        weights_kernel, [((256, 256), BF16), ((8, 128), F32)], scores, other, ids_all, cols, hard
    )
    keep, send = call(
        grad_q_kernel,
        [((144, width), F32), ((128, width), BF16)],
        weights,
        loss,
        *block_p,
        scratch=[((256, width), BF16)],
    )
    got = from_core(send)
    own, opposite = call(
        grad_p_kernel((0, 2)),
        [((64, width), F32), ((64, width), BF16)],
        weights,
        *block_q,
        scratch=[((256, width), BF16)],
    )

    far, loss = call(
        far_sum_kernel, [((48, wide), BF16), ((8, 128), F32)], keep, got, loss, after=[own]
    )
    up, down = call(
        grad_p_kernel((1, 3)),
        [((64, width), BF16)] * 2,
        weights,
        *block_q,
        scratch=[((256, width), BF16)],
        after=[far],
    )
    parts = [from_plane(x, (-dy, 0)) for x, dy in ((up, 1), (opposite, 2), (down, 3))]
    far = from_line(far, 2, back=True)
    near1, near2 = call(near_sum_kernel, [((32, wide), BF16)] * 2, keep, got, far, loss)
    near1, near2 = from_line(near1, 1, back=True), from_line(near2, 2, back=True)
    mine_p, theirs_p = call(row_sum_kernel, [((32, width), F32), ((32, width), BF16)], own, *parts)
    mine, theirs, line = call(
        chip_sum_kernel,
        [((rows, width), F32), ((rows, width), F32), ((NY * NX * 2, 8, 128), F32)],
        keep,
        near1,
        near2,
        loss,
        rel,
        after=[theirs_p],
    )
    line = lax.all_to_all(line, ("y", "xl", "core"), 0, 0, tiled=True)
    mean_loss = (jnp.sum(line[:, 0, :]) / (batch * (batch + per_query))).reshape(1)
    (grad_q,) = call(finish_q_kernel, [((rows, width), BF16)], mine, from_core(theirs))
    grad_p, grad_h = call(finish_p_kernel, [((rows, width), BF16)] * 2, mine_p, from_plane(theirs_p, (0, 1)))
    return mean_loss, grad_q, grad_p, grad_h


def solution(mesh):
    spec = P(DP, "pair")
    return jax.shard_map(
        on_device,
        mesh=Mesh(mesh.devices.reshape(SHAPE), DP + ("pair",)),
        in_specs=(spec, spec, spec, P(DP), P(DP, None)),
        out_specs=(P(), spec, spec, spec),
        check_vma=False,
    )
```

```python
import math

import jax
import jax.numpy as jnp
from jax import lax
from jax.experimental import pallas as pl
from jax.experimental.pallas import tpu as pltpu
from jax.sharding import Mesh, PartitionSpec as P

D = 4096
SCALE = 1.0 / math.sqrt(D)
LOGIT_BIAS = -1.0
BF16, F32, I32 = jnp.bfloat16, jnp.float32, jnp.int32

SHAPE = (4, 2, 8, 2, 2)
DP = ("y", "xl", "z", "core")
PLANE = ("y", "xl")
LINE = ("z", "core")
NY, NX, NZ = 4, 2, 8
STEPS = [(dy, dx) for dy in range(NY) for dx in range(NX)]


def call(kernel, outs, *args, scratch=(), after=()):
    count = len(args)

    def body(*refs):
        kernel(*refs[:count], *refs[count + len(after) :])

    return pl.pallas_call(
        body,
        out_shape=[jax.ShapeDtypeStruct(s, t) for s, t in outs],
        in_specs=[pl.BlockSpec(memory_space=pltpu.VMEM)] * count + [pl.BlockSpec(memory_space=pl.ANY)] * len(after),
        out_specs=[pl.BlockSpec(memory_space=pltpu.VMEM) for _ in outs],
        scratch_shapes=[pltpu.VMEM(s, t) for s, t in scratch],
        compiler_params=pltpu.CompilerParams(vmem_limit_bytes=12 << 20),
    )(*args, *after)


def from_plane(x, step):
    dy, dx = step
    pairs = []
    for y in range(NY):
        for xl in range(NX):
            pairs.append((((y + dy) % NY) * NX + (xl + dx) % NX, y * NX + xl))
    return lax.ppermute(x, PLANE, pairs)


def from_line(x, step, back=False):
    pairs = []
    for z in range(NZ):
        for core in range(2):
            way = step if (core == 0) != back else -step
            pairs.append((((z + way) % NZ) * 2 + core, z * 2 + core))
    return lax.ppermute(x, LINE, pairs)


def from_core(x):
    return lax.ppermute(x, "core", [(0, 1), (1, 0)])


def pack(refs, scratch):
    at, width = 0, scratch.shape[1]
    for ref in refs:
        n = ref.shape[0]
        scratch[at : at + n, :] = ref[:, :width]
        at += n


def lanes3(x, first, shape):
    lane = lax.broadcasted_iota(I32, shape, 1)
    high = x.astype(BF16).astype(F32)
    mid = (x - high).astype(BF16).astype(F32)
    low = (x - high - mid).astype(BF16).astype(F32)
    out = jnp.zeros(shape, F32)
    for i, part in enumerate((high, mid, low)):
        out = jnp.where(lane == first + i, jnp.broadcast_to(part, shape), out)
    return out


def sum_lanes(x, first):
    lane = lax.broadcasted_iota(I32, (1, 128), 1)
    return jnp.sum(jnp.where((lane >= first) & (lane < first + 3), x[:1, :].astype(F32), 0.0), axis=1, keepdims=True)


def own_kernel(q_ref, p_ref, h_ref, pos_ref, hard_ref, own_q, own_p, pos, hard, sems):
    rows, width = q_ref.shape
    moves = [
        (pos_ref, pos),
        (hard_ref, hard),
        (q_ref, own_q.at[:, :width]),
        (p_ref, own_p.at[:rows, :]),
        (h_ref, own_p.at[rows:, :]),
    ]
    copies = [pltpu.make_async_copy(src, dst, sems.at[i]) for i, (src, dst) in enumerate(moves)]
    for copy in copies:
        copy.start()
    copies[0].wait()
    copies[1].wait()
    lane = lax.broadcasted_iota(I32, (8, 128), 1)
    row = lax.broadcasted_iota(I32, (8, 128), 0)
    ids = jnp.zeros((rows, 128), F32)
    first = jnp.broadcast_to(pos[...], (8, rows))
    for shift, part in ((0, lambda v: v // 16), (16, lambda v: v % 16)):
        for values, at in ((hard[...], lane == row + 1 + shift), (first, (lane == shift) & (row == 0))):
            ids = ids + lax.dot_general(
                part(values).astype(F32).astype(BF16),
                jnp.where(at, 1.0, 0.0).astype(BF16),
                (((0,), (0,)), ((), ())),
                preferred_element_type=F32,
            )
    own_q[:, width:] = ids.astype(BF16)
    for copy in copies[2:]:
        copy.wait()


def both_kernel(own_p, other_p, own_q, other_q, row_p, chip_q):
    pack((own_p, other_p), row_p)
    pack((own_q, other_q), chip_q)


def far_kernel(near1, near2, far, both):
    far[:32, :] = near1[...]
    far[32:, :] = near2[:16, :]
    pack((near1, near2), both)


def scores_kernel(*refs):
    q_refs, p_refs, (s_ref, ids_ref, q_all, p_all) = refs[:8], refs[8:14], refs[14:]
    width = p_all.shape[1]
    pack(q_refs, q_all)
    pack(p_refs, p_all)
    at = 0
    for ref in q_refs:
        n = ref.shape[0]
        ids_ref[at : at + n, :] = ref[:, width:]
        at += n
    s_ref[...] = lax.dot_general(q_all[...], p_all[...], (((1,), (1,)), ((), ())), preferred_element_type=F32)


def weights_kernel(s_ref, got_ref, ids_ref, cols_ref, hard_ref, w_ref, loss_ref):
    logits = SCALE * (s_ref[...] + got_ref[...]) + LOGIT_BIAS
    col = jnp.broadcast_to(cols_ref[...], logits.shape)
    hard = jnp.broadcast_to(hard_ref[...], logits.shape) > 0.0
    ids = ids_ref[...].astype(F32)

    def hits(k):
        return (ids[:, k : k + 1] * 16.0 + ids[:, 16 + k : 17 + k] == col).astype(F32)

    labels = hits(0)
    counts = hits(1)
    for k in range(2, 9):
        counts = counts + hits(k)
    e = jnp.exp(-jnp.abs(logits))
    sigmoid = jnp.where(logits >= 0.0, 1.0, e) / (1.0 + e)
    softplus = jnp.maximum(logits, 0.0) + jnp.log1p(e)
    in_batch = ((sigmoid - labels) * SCALE).astype(BF16)
    picked = (counts * (sigmoid * SCALE).astype(BF16).astype(F32)).astype(BF16)
    w_ref[...] = jnp.where(hard, picked, in_batch)
    loss = jnp.sum(jnp.where(hard, counts * softplus, softplus - labels * logits), axis=1, keepdims=True)
    loss = jnp.sum(loss, axis=0, keepdims=True)
    loss_ref[...] = jnp.broadcast_to(loss, loss_ref.shape)


def grad_q_kernel(w_ref, loss_ref, *refs):
    p_refs, (keep_ref, send_ref, p_all) = refs[:6], refs[6:]
    pack(p_refs, p_all)
    part = jnp.dot(w_ref[...], p_all[...], preferred_element_type=F32)
    keep_ref[...] = part[:144, :]
    send_ref[:112, :] = part[144:, :].astype(BF16)
    send_ref[112:, :128] = lanes3(loss_ref[:1, :1], 0, (16, 128)).astype(BF16)
    send_ref[112:, 128:] = jnp.zeros((16, send_ref.shape[1] - 128), BF16)


def grad_p_kernel(w_ref, *refs):
    q_refs, p_outs, q_all = refs[:8], refs[8:12], refs[12]
    pack(q_refs, q_all)
    part = lax.dot_general(w_ref[...], q_all[...], (((0,), (0,)), ((), ())), preferred_element_type=F32)
    for k, ref in enumerate(p_outs):
        ref[...] = part[64 * k : 64 * k + 64, :].astype(ref.dtype)


def far_sum_kernel(keep_ref, got_ref, loss_ref, far_ref, chip_loss_ref):
    width = keep_ref.shape[1]
    loss = loss_ref[:1, :1] + sum_lanes(got_ref[112:, :128], 0)
    chip_loss_ref[...] = jnp.broadcast_to(loss, chip_loss_ref.shape)
    far_ref[:, :width] = (keep_ref[96:144, :] + got_ref[64:112, :].astype(F32)).astype(BF16)
    far_ref[:, width:] = lanes3(loss, 0, (48, 128)).astype(BF16)


def near_sum_kernel(keep_ref, got_ref, far_ref, loss_ref, near1_ref, near2_ref):
    width = keep_ref.shape[1]
    far_loss = sum_lanes(far_ref[:16, width:], 0)
    lanes = (lanes3(loss_ref[:1, :1], 0, (32, 128)) + lanes3(far_loss, 3, (32, 128))).astype(BF16)
    near1_ref[:, width:] = lanes
    near2_ref[:, width:] = lanes
    near1 = keep_ref[32:64, :] + got_ref[:32, :].astype(F32) + far_ref[:32, :width].astype(F32)
    near1_ref[:, :width] = near1.astype(BF16)
    near2 = keep_ref[64:80, :] + got_ref[32:48, :].astype(F32) + far_ref[32:, :width].astype(F32)
    near2_ref[:16, :width] = near2.astype(BF16)
    near2_ref[16:, :width] = (keep_ref[80:96, :] + got_ref[48:64, :].astype(F32)).astype(BF16)


def chip_sum_kernel(keep_ref, b1, b2, loss_ref, rel_ref, mine_ref, theirs_ref, line_ref):
    rows, width = mine_ref.shape
    rel = rel_ref[...]
    line = jnp.where(rel == 0, loss_ref[:1, :1], 0.0)
    for step, ref, first in ((1, b1, 0), (3, b1, 3), (2, b2, 0), (4, b2, 3)):
        line = jnp.where(rel == step, sum_lanes(ref[:16, width:], first), line)
    line_ref[...] = jnp.broadcast_to(line[None], line_ref.shape)
    total = keep_ref[: 2 * rows, :] + b1[:, :width].astype(F32) + b2[:, :width].astype(F32)
    mine_ref[...] = total[:rows, :]
    theirs_ref[...] = total[rows:, :]


def row_sum_kernel(own_ref, b1, b2, b3, mine_ref, theirs_ref):
    total = own_ref[...]
    for ref in (b1, b2, b3):
        total = total + ref[...].astype(F32)
    mine_ref[...] = total[:32, :]
    theirs_ref[...] = total[32:, :].astype(BF16)


def finish_kernel(count):
    def kernel(mine_q, got_q, mine_p, got_p, line_ref, q_ref, p_ref, h_ref, loss_ref):
        rows = q_ref.shape[0]
        q_ref[...] = (mine_q[...] + got_q[...]).astype(BF16)
        total = mine_p[...] + got_p[...].astype(F32)
        p_ref[...] = total[:rows, :].astype(BF16)
        h_ref[...] = total[rows:, :].astype(BF16)
        line = jnp.sum(line_ref[...], axis=0)[:1, :]
        loss_ref[...] = jnp.sum(line, axis=1, keepdims=True) / count

    return kernel


def on_device(queries, passages, hard_passages, positive_ids, hard_ids):
    rows, width = queries.shape
    wide = width + 128
    batch = rows * NY * NX * NZ * 2
    per_query = hard_ids.shape[1]
    core, z = lax.axis_index("core"), lax.axis_index("z")

    own_q, own_p = pl.pallas_call(
        own_kernel,
        out_shape=[jax.ShapeDtypeStruct((rows, wide), BF16), jax.ShapeDtypeStruct((2 * rows, width), BF16)],
        in_specs=[pl.BlockSpec(memory_space=pltpu.HBM)] * 5,
        out_specs=[pl.BlockSpec(memory_space=pltpu.VMEM)] * 2,
        scratch_shapes=[pltpu.VMEM((1, rows), I32), pltpu.VMEM((per_query, rows), I32), pltpu.SemaphoreType.DMA((5,))],
        compiler_params=pltpu.CompilerParams(vmem_limit_bytes=12 << 20),
    )(
        *(
            pltpu.with_memory_space_constraint(x, pltpu.HBM)
            for x in (queries, passages, hard_passages, positive_ids.reshape(1, rows), hard_ids.T)
        )
    )
    other_p = from_plane(own_p, (0, 1))
    row_p, chip_q = call(
        both_kernel,
        [((4 * rows, width), BF16), ((2 * rows, wide), BF16)],
        own_p,
        other_p,
        own_q,
        from_core(own_q),
    )
    own_up, own_down = from_plane(own_p, (1, 0)), from_plane(own_p, (3, 0))
    other_up, other_down = from_plane(other_p, (1, 0)), from_plane(other_p, (3, 0))
    block_p = [row_p, own_up, other_up, from_plane(row_p, (2, 0)), own_down, other_down]
    near1, near2 = from_line(chip_q, 1), from_line(chip_q, 2)
    far, both = call(
        far_kernel, [((48, wide), BF16), ((64, wide), BF16)], near1, near2, after=[own_up, own_down]
    )
    far = from_line(far, 2)
    far_parts = [from_core(far[at : at + 16]) for at in (0, 16, 32)]
    block_q = [chip_q, near1, near2, far, from_core(both), *far_parts]

    place = jnp.arange(32, dtype=I32)
    owners = []
    for dy, dx in STEPS:
        y = (lax.axis_index("y") + dy) % NY
        x = (lax.axis_index("xl") + dx) % NX
        owners.append((y * NX + x) * (NZ * 2) + lax.axis_index(LINE))
    owners = jnp.stack(owners)
    cols = (owners[:, None] * rows + place[None, :] % rows).reshape(1, 256).astype(F32)
    hard = jnp.broadcast_to(place[None, :] >= rows, (8, 32)).reshape(1, 256).astype(F32)
    lane = jnp.arange(128, dtype=I32)[None, :]
    rel = jnp.where(lane < NZ, jnp.where(core == 0, z - lane, lane - z) % NZ, NZ)
    rel = jnp.where((core == 1) & (rel % 4 == 0), NZ, rel)

    scores, ids_all = call(
        scores_kernel,
        [((256, 256), F32), ((256, 128), BF16)],
        *block_q,
        *block_p,
        scratch=[((256, width), BF16), ((256, width), BF16)],
    )
    other = lax.ppermute(scores, "pair", [(0, 1), (1, 0)])
    weights, loss = call(
        weights_kernel, [((256, 256), BF16), ((8, 128), F32)], scores, other, ids_all, cols, hard
    )
    keep, send = call(
        grad_q_kernel,
        [((144, width), F32), ((128, width), BF16)],
        weights,
        loss,
        *block_p,
        scratch=[((256, width), BF16)],
    )
    got = from_core(send)
    far, loss = call(far_sum_kernel, [((48, wide), BF16), ((8, 128), F32)], keep, got, loss)
    own, *rest = call(
        grad_p_kernel,
        [((64, width), F32)] + [((64, width), BF16)] * 3,
        weights,
        *block_q,
        scratch=[((256, width), BF16)],
        after=[far],
    )
    parts = [from_plane(x, (-dy, 0)) for x, dy in zip(rest, (1, 2, 3))]
    far = from_line(far, 2, back=True)
    near1, near2 = call(near_sum_kernel, [((32, wide), BF16)] * 2, keep, got, far, loss)
    near1, near2 = from_line(near1, 1, back=True), from_line(near2, 2, back=True)
    mine_p, theirs_p = call(row_sum_kernel, [((32, width), F32), ((32, width), BF16)], own, *parts)
    mine, theirs, line = call(
        chip_sum_kernel,
        [((rows, width), F32), ((rows, width), F32), ((NY * NX * 2, 8, 128), F32)],
        keep,
        near1,
        near2,
        loss,
        rel,
        after=[theirs_p],
    )
    line = lax.all_to_all(line, ("y", "xl", "core"), 0, 0, tiled=True)
    grad_q, grad_p, grad_h, mean_loss = call(
        finish_kernel(batch * (batch + per_query)),
        [((rows, width), BF16)] * 3 + [((1, 1), F32)],
        mine,
        from_core(theirs),
        mine_p,
        from_plane(theirs_p, (0, 1)),
        line,
    )
    return mean_loss.reshape(1), grad_q, grad_p, grad_h


def solution(mesh):
    spec = P(DP, "pair")
    return jax.shard_map(
        on_device,
        mesh=Mesh(mesh.devices.reshape(SHAPE), DP + ("pair",)),
        in_specs=(spec, spec, spec, P(DP), P(DP, None)),
        out_specs=(P(), spec, spec, spec),
        check_vma=False,
    )
```

```python
import math

import jax
import jax.numpy as jnp
from jax import lax
from jax.experimental import pallas as pl
from jax.experimental.pallas import tpu as pltpu
from jax.sharding import Mesh, PartitionSpec as P

D = 4096
SCALE = 1.0 / math.sqrt(D)
LOGIT_BIAS = -1.0
BF16, F32, I32 = jnp.bfloat16, jnp.float32, jnp.int32

SHAPE = (4, 2, 8, 2, 2)
DP = ("y", "xl", "z", "core")
PLANE = ("y", "xl")
LINE = ("z", "core")
NY, NX, NZ = 4, 2, 8


def call(kernel, outs, *args, scratch=(), after=(), final=False):
    count = len(args)

    def body(*refs):
        kernel(*refs[:count], *refs[count + len(after) :])

    return pl.pallas_call(
        body,
        out_shape=[jax.ShapeDtypeStruct(s, t) if final else pltpu.VMEM(s, t) for s, t in outs],
        in_specs=[pl.BlockSpec(memory_space=pltpu.VMEM)] * count + [pl.BlockSpec(memory_space=pl.ANY)] * len(after),
        out_specs=[pl.BlockSpec(memory_space=pltpu.VMEM) for _ in outs],
        scratch_shapes=[pltpu.VMEM(s, t) for s, t in scratch],
        compiler_params=pltpu.CompilerParams(vmem_limit_bytes=12 << 20),
    )(*args, *after)


def from_plane(x, step):
    dy, dx = step
    pairs = []
    for y in range(NY):
        for xl in range(NX):
            pairs.append((((y + dy) % NY) * NX + (xl + dx) % NX, y * NX + xl))
    return lax.ppermute(x, PLANE, pairs)


def from_line(x, step, back=False):
    pairs = []
    for z in range(NZ):
        for core in range(2):
            way = step if (core == 0) != back else -step
            pairs.append((((z + way) % NZ) * 2 + core, z * 2 + core))
    return lax.ppermute(x, LINE, pairs)


def from_core(x):
    return lax.ppermute(x, "core", [(0, 1), (1, 0)])


def pack(refs, scratch):
    at, width = 0, scratch.shape[1]
    for ref in refs:
        n = ref.shape[0]
        scratch[at : at + n, :] = ref[:, :width]
        at += n


def lanes3(x, first, shape):
    lane = lax.broadcasted_iota(I32, shape, 1)
    high = x.astype(BF16).astype(F32)
    mid = (x - high).astype(BF16).astype(F32)
    low = (x - high - mid).astype(BF16).astype(F32)
    out = jnp.zeros(shape, F32)
    for i, part in enumerate((high, mid, low)):
        out = jnp.where(lane == first + i, jnp.broadcast_to(part, shape), out)
    return out


def sum_lanes(x, first):
    lane = lax.broadcasted_iota(I32, (1, 128), 1)
    return jnp.sum(jnp.where((lane >= first) & (lane < first + 3), x[:1, :].astype(F32), 0.0), axis=1, keepdims=True)


def own_kernel(at_ref, q_ref, p_ref, h_ref, pos_ref, hard_ref, own_q, own_p, cols_ref, rel_ref, pos, hard, sems):
    rows, width = q_ref.shape
    moves = [
        (pos_ref, pos),
        (hard_ref, hard),
        (q_ref, own_q.at[:, :width]),
        (p_ref, own_p.at[:rows, :]),
        (h_ref, own_p.at[rows:, :]),
    ]
    copies = [pltpu.make_async_copy(src, dst, sems.at[i]) for i, (src, dst) in enumerate(moves)]
    for copy in copies:
        copy.start()
    copies[0].wait()
    copies[1].wait()
    lane = lax.broadcasted_iota(I32, (8, 128), 1)
    row = lax.broadcasted_iota(I32, (8, 128), 0)
    ids = jnp.zeros((rows, 128), F32)
    first = jnp.broadcast_to(pos[...], (8, rows))
    for shift, part in ((0, lambda v: v >> 4), (16, lambda v: v & 15)):
        for values, at in ((hard[...], lane == row + 1 + shift), (first, (lane == shift) & (row == 0))):
            ids = ids + lax.dot_general(
                part(values).astype(F32).astype(BF16),
                jnp.where(at, 1.0, 0.0).astype(BF16),
                (((0,), (0,)), ((), ())),
                preferred_element_type=F32,
            )
    own_q[:, width:] = ids.astype(BF16)

    lane = lax.broadcasted_iota(I32, (8, 256), 1)
    y = (at_ref[0] + (lane >> 6)) & (NY - 1)
    x = (at_ref[1] + (lane >> 5)) & (NX - 1)
    owner = (y * NX + x) * (NZ * 2) + at_ref[2] * 2 + at_ref[3]
    row = lax.broadcasted_iota(I32, (8, 256), 0)
    cols_ref[...] = jnp.where(row == 0, owner * 16 + (lane & 15), (lane >> 4) & 1).astype(F32)
    lane = lax.broadcasted_iota(I32, (8, 128), 1)
    rel = jnp.where(at_ref[3] == 0, at_ref[2] - lane, lane - at_ref[2]) & (NZ - 1)
    rel_ref[...] = jnp.where((lane >= NZ) | ((at_ref[3] == 1) & ((rel & 3) == 0)), NZ, rel)
    for copy in copies[2:]:
        copy.wait()


def pack_kernel(*refs):
    pack(refs[:-1], refs[-1])


def split_kernel(ref, *parts):
    for i, part in enumerate(parts):
        part[...] = ref[16 * i : 16 * i + 16, :]


def far_kernel(near1, near2, far):
    far[:32, :] = near1[...]
    far[32:, :] = near2[:16, :]


def near_scores_kernel(*refs):
    q_refs, p_refs, (s_ref, ids_ref, q_all, p_all) = refs[:4], refs[4:12], refs[12:]
    width = p_all.shape[1]
    pack(q_refs, q_all)
    pack(p_refs, p_all)
    at = 0
    for ref in q_refs:
        n = ref.shape[0]
        ids_ref[at : at + n, :] = ref[:, width:]
        at += n
    s_ref[...] = lax.dot_general(q_all[...], p_all[...], (((1,), (1,)), ((), ())), preferred_element_type=F32)


def far_scores_kernel(*refs):
    q_refs, (p_all, s_ref, ids_ref, q_all) = refs[:4], refs[4:]
    width = p_all.shape[1]
    pack(q_refs, q_all)
    at = 0
    for ref in q_refs:
        n = ref.shape[0]
        ids_ref[at : at + n, :] = ref[:, width:]
        at += n
    s_ref[...] = lax.dot_general(q_all[...], p_all[...], (((1,), (1,)), ((), ())), preferred_element_type=F32)


def weights_kernel(s_near, s_far, got_near, got_far, ids_near, ids_far, cols_ref, w_near, w_far, loss_ref):
    near = s_near.shape[0]
    scores = jnp.concatenate([s_near[...] + got_near[...], s_far[...] + got_far[...]], axis=0)
    logits = SCALE * scores + LOGIT_BIAS
    ids = jnp.concatenate([ids_near[...].astype(F32), ids_far[...].astype(F32)], axis=0)
    col = jnp.broadcast_to(cols_ref[:1, :], logits.shape)
    hard = jnp.broadcast_to(cols_ref[1:2, :], logits.shape) > 0.0

    def hits(k):
        return (ids[:, k : k + 1] * 16.0 + ids[:, 16 + k : 17 + k] == col).astype(F32)

    labels = hits(0)
    counts = hits(1)
    for k in range(2, 9):
        counts = counts + hits(k)
    e = jnp.exp(-jnp.abs(logits))
    sigmoid = jnp.where(logits >= 0.0, 1.0, e) / (1.0 + e)
    softplus = jnp.maximum(logits, 0.0) + jnp.log1p(e)
    in_batch = ((sigmoid - labels) * SCALE).astype(BF16)
    picked = (counts * (sigmoid * SCALE).astype(BF16).astype(F32)).astype(BF16)
    weights = jnp.where(hard, picked, in_batch)
    w_near[...] = weights[:near, :]
    w_far[...] = weights[near:, :]
    loss = jnp.sum(jnp.where(hard, counts * softplus, softplus - labels * logits), axis=1, keepdims=True)
    loss = jnp.sum(loss, axis=0, keepdims=True)
    loss_ref[...] = jnp.broadcast_to(loss, loss_ref.shape)


def grad_q_kernel(w_near, w_far, p_all, loss_ref, keep_ref, send_ref):
    near = jnp.dot(w_near[...], p_all[...], preferred_element_type=F32)
    far = jnp.dot(w_far[...], p_all[...], preferred_element_type=F32)
    keep_ref[:96, :] = near[:96, :]
    keep_ref[96:, :] = far[:48, :]
    send_ref[:64, :] = near[96:, :].astype(BF16)
    send_ref[64:112, :] = far[48:, :].astype(BF16)
    send_ref[112:, :128] = lanes3(loss_ref[:1, :1], 0, (16, 128)).astype(BF16)
    send_ref[112:, 128:] = jnp.zeros((16, send_ref.shape[1] - 128), BF16)


def grad_p_kernel(w_near, w_far, q_near, q_far, *p_outs):
    across = (((0,), (0,)), ((), ()))
    part = lax.dot_general(w_near[...], q_near[...], across, preferred_element_type=F32)
    part = part + lax.dot_general(w_far[...], q_far[...], across, preferred_element_type=F32)
    for k, ref in enumerate(p_outs):
        ref[...] = part[64 * k : 64 * k + 64, :].astype(ref.dtype)


def far_sum_kernel(keep_ref, got_ref, loss_ref, far_ref, chip_loss_ref):
    width = keep_ref.shape[1]
    loss = loss_ref[:1, :1] + sum_lanes(got_ref[112:, :128], 0)
    chip_loss_ref[...] = jnp.broadcast_to(loss, chip_loss_ref.shape)
    far_ref[:, :width] = (keep_ref[96:144, :] + got_ref[64:112, :].astype(F32)).astype(BF16)
    far_ref[:, width:] = lanes3(loss, 0, (48, 128)).astype(BF16)


def near_sum_kernel(keep_ref, got_ref, far_ref, loss_ref, near1_ref, near2_ref):
    width = keep_ref.shape[1]
    far_loss = sum_lanes(far_ref[:16, width:], 0)
    lanes = (lanes3(loss_ref[:1, :1], 0, (32, 128)) + lanes3(far_loss, 3, (32, 128))).astype(BF16)
    near1_ref[:, width:] = lanes
    near2_ref[:, width:] = lanes
    near1 = keep_ref[32:64, :] + got_ref[:32, :].astype(F32) + far_ref[:32, :width].astype(F32)
    near1_ref[:, :width] = near1.astype(BF16)
    near2 = keep_ref[64:80, :] + got_ref[32:48, :].astype(F32) + far_ref[32:, :width].astype(F32)
    near2_ref[:16, :width] = near2.astype(BF16)
    near2_ref[16:, :width] = (keep_ref[80:96, :] + got_ref[48:64, :].astype(F32)).astype(BF16)


def chip_sum_kernel(keep_ref, b1, b2, loss_ref, rel_ref, mine_ref, theirs_ref, line_ref):
    rows, width = mine_ref.shape
    rel = rel_ref[:1, :]
    line = jnp.where(rel == 0, loss_ref[:1, :1], 0.0)
    for step, ref, first in ((1, b1, 0), (3, b1, 3), (2, b2, 0), (4, b2, 3)):
        line = jnp.where(rel == step, sum_lanes(ref[:16, width:], first), line)
    line_ref[...] = jnp.broadcast_to(line[None], line_ref.shape)
    total = keep_ref[: 2 * rows, :] + b1[:, :width].astype(F32) + b2[:, :width].astype(F32)
    mine_ref[...] = total[:rows, :]
    theirs_ref[...] = total[rows:, :]


def row_sum_kernel(own_ref, b1, b2, b3, mine_ref, theirs_ref):
    total = own_ref[...]
    for ref in (b1, b2, b3):
        total = total + ref[...].astype(F32)
    mine_ref[...] = total[:32, :]
    theirs_ref[...] = total[32:, :].astype(BF16)


def finish_kernel(count):
    def kernel(mine_q, got_q, mine_p, got_p, line_ref, q_ref, p_ref, h_ref, loss_ref):
        rows = q_ref.shape[0]
        q_ref[...] = (mine_q[...] + got_q[...]).astype(BF16)
        total = mine_p[...] + got_p[...].astype(F32)
        p_ref[...] = total[:rows, :].astype(BF16)
        h_ref[...] = total[rows:, :].astype(BF16)
        line = jnp.sum(line_ref[...], axis=0)[:1, :]
        loss_ref[...] = jnp.sum(line, axis=1, keepdims=True) / count

    return kernel


def on_device(queries, passages, hard_passages, positive_ids, hard_ids):
    rows, width = queries.shape
    wide = width + 128
    batch = rows * NY * NX * NZ * 2
    per_query = hard_ids.shape[1]

    place = jnp.stack([lax.axis_index(name) for name in DP])
    own_q, own_p, cols, rel = pl.pallas_call(
        own_kernel,
        out_shape=[
            pltpu.VMEM((rows, wide), BF16),
            pltpu.VMEM((2 * rows, width), BF16),
            pltpu.VMEM((8, 256), F32),
            pltpu.VMEM((8, 128), I32),
        ],
        in_specs=[pl.BlockSpec(memory_space=pltpu.SMEM)] + [pl.BlockSpec(memory_space=pltpu.HBM)] * 5,
        out_specs=[pl.BlockSpec(memory_space=pltpu.VMEM)] * 4,
        scratch_shapes=[pltpu.VMEM((1, rows), I32), pltpu.VMEM((per_query, rows), I32), pltpu.SemaphoreType.DMA((5,))],
        compiler_params=pltpu.CompilerParams(vmem_limit_bytes=12 << 20),
    )(
        place,
        *(
            pltpu.with_memory_space_constraint(x, pltpu.HBM)
            for x in (queries, passages, hard_passages, positive_ids.reshape(1, rows), hard_ids.T)
        ),
    )
    other_p = from_plane(own_p, (0, 1))
    (chip_q,) = call(pack_kernel, [((2 * rows, wide), BF16)], own_q, from_core(own_q))
    own_up, own_down = from_plane(own_p, (1, 0)), from_plane(own_p, (3, 0))
    other_up, other_down = from_plane(other_p, (1, 0)), from_plane(other_p, (3, 0))
    own_opposite = from_plane(own_p, (2, 0))
    other_opposite = from_plane(own_opposite, (0, 1))
    block_p = [own_p, other_p, own_up, other_up, own_opposite, other_opposite, own_down, other_down]
    near1, near2 = from_line(chip_q, 1), from_line(chip_q, 2)
    (far,) = call(far_kernel, [((48, wide), BF16)], near1, near2, after=[other_p, own_up, own_down])
    (both,) = call(pack_kernel, [((64, wide), BF16)], near1, near2, after=[own_opposite])
    far = from_line(far, 2)
    far_parts = [from_core(x) for x in call(split_kernel, [((16, wide), BF16)] * 3, far)]

    near, rest = 160, 96
    s_near, ids_near, q_near, p_all = call(
        near_scores_kernel,
        [((near, 256), F32), ((near, 128), BF16), ((near, width), BF16), ((256, width), BF16)],
        chip_q,
        near1,
        near2,
        from_core(both),
        *block_p,
    )
    s_far, ids_far, q_far = call(
        far_scores_kernel,
        [((rest, 256), F32), ((rest, 128), BF16), ((rest, width), BF16)],
        far,
        *far_parts,
        p_all,
    )
    swap = [(0, 1), (1, 0)]
    w_near, w_far, loss = call(
        weights_kernel,
        [((near, 256), BF16), ((rest, 256), BF16), ((8, 128), F32)],
        s_near,
        s_far,
        lax.ppermute(s_near, "pair", swap),
        lax.ppermute(s_far, "pair", swap),
        ids_near,
        ids_far,
        cols,
    )
    keep, send = call(
        grad_q_kernel, [((144, width), F32), ((128, width), BF16)], w_near, w_far, p_all, loss
    )
    got = from_core(send)
    far, loss = call(far_sum_kernel, [((48, wide), BF16), ((8, 128), F32)], keep, got, loss)
    own, *rest = call(
        grad_p_kernel,
        [((64, width), F32)] + [((64, width), BF16)] * 3,
        w_near,
        w_far,
        q_near,
        q_far,
        after=[far],
    )
    parts = [from_plane(x, (-dy, 0)) for x, dy in zip(rest, (1, 2, 3))]
    far = from_line(far, 2, back=True)
    near1, near2 = call(near_sum_kernel, [((32, wide), BF16)] * 2, keep, got, far, loss)
    near1, near2 = from_line(near1, 1, back=True), from_line(near2, 2, back=True)
    mine_p, theirs_p = call(row_sum_kernel, [((32, width), F32), ((32, width), BF16)], own, *parts)
    mine, theirs, line = call(
        chip_sum_kernel,
        [((rows, width), F32), ((rows, width), F32), ((NY * NX * 2, 8, 128), F32)],
        keep,
        near1,
        near2,
        loss,
        rel,
        after=[theirs_p],
    )
    line = lax.all_to_all(line, ("y", "xl", "core"), 0, 0, tiled=True)
    grad_q, grad_p, grad_h, mean_loss = call(
        finish_kernel(batch * (batch + per_query)),
        [((rows, width), BF16)] * 3 + [((1, 1), F32)],
        mine,
        from_core(theirs),
        mine_p,
        from_plane(theirs_p, (0, 1)),
        line,
        final=True,
    )
    return mean_loss.reshape(1), grad_q, grad_p, grad_h


def solution(mesh):
    spec = P(DP, "pair")
    return jax.shard_map(
        on_device,
        mesh=Mesh(mesh.devices.reshape(SHAPE), DP + ("pair",)),
        in_specs=(spec, spec, spec, P(DP), P(DP, None)),
        out_specs=(P(), spec, spec, spec),
        check_vma=False,
    )
```

```python
import math

import jax
import jax.numpy as jnp
from jax import lax
from jax.experimental import pallas as pl
from jax.experimental.pallas import tpu as pltpu
from jax.sharding import Mesh, PartitionSpec as P

D = 4096
SCALE = 1.0 / math.sqrt(D)
LOGIT_BIAS = -1.0
BF16, F32, I32 = jnp.bfloat16, jnp.float32, jnp.int32

SHAPE = (4, 2, 8, 2, 2)
DP = ("y", "xl", "z", "core")
PLANE = ("y", "xl")
LINE = ("z", "core")
NY, NX, NZ = 4, 2, 8
LINE_ROWS = 12


def call(kernel, outs, *args, scratch=(), after=(), final=False):
    count = len(args)

    def body(*refs):
        kernel(*refs[:count], *refs[count + len(after) :])

    return pl.pallas_call(
        body,
        out_shape=[jax.ShapeDtypeStruct(s, t) if final else pltpu.VMEM(s, t) for s, t in outs],
        in_specs=[pl.BlockSpec(memory_space=pltpu.VMEM)] * count + [pl.BlockSpec(memory_space=pl.ANY)] * len(after),
        out_specs=[pl.BlockSpec(memory_space=pltpu.VMEM) for _ in outs],
        scratch_shapes=[pltpu.VMEM(s, t) for s, t in scratch],
        compiler_params=pltpu.CompilerParams(vmem_limit_bytes=12 << 20),
    )(*args, *after)


def from_plane(x, step):
    dy, dx = step
    pairs = []
    for y in range(NY):
        for xl in range(NX):
            pairs.append((((y + dy) % NY) * NX + (xl + dx) % NX, y * NX + xl))
    return lax.ppermute(x, PLANE, pairs)


def from_line(x, step, back=False):
    pairs = []
    for z in range(NZ):
        for core in range(2):
            way = step if (core == 0) != back else -step
            pairs.append((((z + way) % NZ) * 2 + core, z * 2 + core))
    return lax.ppermute(x, LINE, pairs)


def from_core(x):
    return lax.ppermute(x, "core", [(0, 1), (1, 0)])


def pack(refs, scratch):
    at, width = 0, scratch.shape[1]
    for ref in refs:
        n = ref.shape[0]
        scratch[at : at + n, :] = ref[:, :width]
        at += n


def lanes3(x, first, shape):
    lane = lax.broadcasted_iota(I32, shape, 1)
    high = x.astype(BF16).astype(F32)
    mid = (x - high).astype(BF16).astype(F32)
    low = (x - high - mid).astype(BF16).astype(F32)
    out = jnp.zeros(shape, F32)
    for i, part in enumerate((high, mid, low)):
        out = jnp.where(lane == first + i, jnp.broadcast_to(part, shape), out)
    return out


def sum_lanes(x, first):
    lane = lax.broadcasted_iota(I32, (1, 128), 1)
    return jnp.sum(jnp.where((lane >= first) & (lane < first + 3), x[:1, :].astype(F32), 0.0), axis=1, keepdims=True)


def own_kernel(q_ref, p_ref, h_ref, pos_ref, hard_ref, own_q, own_p, pos, hard, sems):
    rows, width = q_ref.shape
    moves = [
        (pos_ref, pos),
        (hard_ref, hard),
        (q_ref, own_q.at[:, :width]),
        (p_ref, own_p.at[:rows, :]),
        (h_ref, own_p.at[rows:, :]),
    ]
    copies = [pltpu.make_async_copy(src, dst, sems.at[i]) for i, (src, dst) in enumerate(moves)]
    for copy in copies:
        copy.start()
    copies[0].wait()
    copies[1].wait()
    lane = lax.broadcasted_iota(I32, (8, 128), 1)
    row = lax.broadcasted_iota(I32, (8, 128), 0)
    ids = jnp.zeros((rows, 128), F32)
    first = jnp.broadcast_to(pos[...], (8, rows))
    for shift, part in ((0, lambda v: v >> 4), (16, lambda v: v & 15)):
        for values, at in ((hard[...], lane == row + 1 + shift), (first, (lane == shift) & (row == 0))):
            ids = ids + lax.dot_general(
                part(values).astype(F32).astype(BF16),
                jnp.where(at, 1.0, 0.0).astype(BF16),
                (((0,), (0,)), ((), ())),
                preferred_element_type=F32,
            )
    own_q[:, width:] = ids.astype(BF16)
    for copy in copies[2:]:
        copy.wait()


def place_kernel(at_ref, cols_ref, rel_ref):
    lane = lax.broadcasted_iota(I32, (8, 256), 1)
    y = (at_ref[0] + (lane >> 6)) & (NY - 1)
    x = (at_ref[1] + (lane >> 5)) & (NX - 1)
    owner = (y * NX + x) * (NZ * 2) + at_ref[2] * 2 + at_ref[3]
    row = lax.broadcasted_iota(I32, (8, 256), 0)
    cols_ref[...] = jnp.where(row == 0, owner * 16 + (lane & 15), (lane >> 4) & 1).astype(F32)
    lane = lax.broadcasted_iota(I32, (8, 128), 1)
    rel = jnp.where(at_ref[3] == 0, at_ref[2] - lane, lane - at_ref[2]) & (NZ - 1)
    rel_ref[...] = jnp.where((lane >= NZ) | ((at_ref[3] == 1) & ((rel & 3) == 0)), NZ, rel)


def pack_kernel(*refs):
    pack(refs[:-1], refs[-1])


def split_kernel(ref, *parts):
    for i, part in enumerate(parts):
        part[...] = ref[16 * i : 16 * i + 16, :]


def far_kernel(near1, near2, far):
    far[:32, :] = near1[...]
    far[32:, :] = near2[:16, :]


def scores_kernel(*refs):
    q_refs, p_refs, (s_ref, ids_ref, q_all, p_all) = refs[:8], refs[8:16], refs[16:]
    width = p_all.shape[1]
    pack(q_refs, q_all)
    pack(p_refs, p_all)
    at = 0
    for ref in q_refs:
        n = ref.shape[0]
        ids_ref[at : at + n, :] = ref[:, width:]
        at += n
    s_ref[...] = lax.dot_general(q_all[...], p_all[...], (((1,), (1,)), ((), ())), preferred_element_type=F32)


def weights_kernel(s_ref, got_ref, ids_ref, cols_ref, w_ref, loss_ref):
    logits = SCALE * (s_ref[...] + got_ref[...]) + LOGIT_BIAS
    ids = ids_ref[...].astype(F32)
    col = jnp.broadcast_to(cols_ref[:1, :], logits.shape)
    hard = jnp.broadcast_to(cols_ref[1:2, :], logits.shape) > 0.0

    ids = ids[:, :16] * 16.0 + ids[:, 16:32]

    def hits(k):
        return (ids[:, k : k + 1] == col).astype(F32)

    labels = hits(0)
    counts = hits(1)
    for k in range(2, 9):
        counts = counts + hits(k)
    e = jnp.exp(-jnp.abs(logits))
    sigmoid = jnp.where(logits >= 0.0, 1.0, e) / (1.0 + e)
    softplus = jnp.maximum(logits, 0.0) + jnp.log1p(e)
    in_batch = ((sigmoid - labels) * SCALE).astype(BF16)
    picked = (counts * (sigmoid * SCALE).astype(BF16).astype(F32)).astype(BF16)
    w_ref[...] = jnp.where(hard, picked, in_batch)
    loss = jnp.sum(jnp.where(hard, counts * softplus, softplus - labels * logits), axis=1, keepdims=True)
    loss = jnp.sum(loss, axis=0, keepdims=True)
    loss_ref[...] = jnp.broadcast_to(loss, loss_ref.shape)


def grad_q_kernel(w_ref, p_all, loss_ref, keep_ref, send_ref):
    part = jnp.dot(w_ref[...], p_all[...], preferred_element_type=F32)
    keep_ref[...] = part[:144, :]
    send_ref[:112, :] = part[144:, :].astype(BF16)
    send_ref[112:, :128] = lanes3(loss_ref[:1, :1], 0, (16, 128)).astype(BF16)
    send_ref[112:, 128:] = jnp.zeros((16, send_ref.shape[1] - 128), BF16)


def grad_p_kernel(w_ref, q_all, own_ref, up_ref, down_ref, opposite_ref, other_ref):
    part = lax.dot_general(w_ref[...], q_all[...], (((0,), (0,)), ((), ())), preferred_element_type=F32)
    own_ref[...] = part[:64, :]
    up_ref[...] = part[64:128, :].astype(BF16)
    opposite_ref[...] = part[128:160, :]
    other_ref[...] = part[160:192, :].astype(BF16)
    down_ref[...] = part[192:, :].astype(BF16)


def opposite_kernel(mine_ref, got_ref, out_ref):
    out_ref[...] = (mine_ref[...] + got_ref[...].astype(F32)).astype(BF16)


def far_sum_kernel(keep_ref, got_ref, loss_ref, far_ref, chip_loss_ref):
    width = keep_ref.shape[1]
    loss = loss_ref[:1, :1] + sum_lanes(got_ref[112:, :128], 0)
    chip_loss_ref[...] = jnp.broadcast_to(loss, chip_loss_ref.shape)
    far_ref[:, :width] = (keep_ref[96:144, :] + got_ref[64:112, :].astype(F32)).astype(BF16)
    far_ref[:, width:] = lanes3(loss, 0, (48, 128)).astype(BF16)


def near_sum_kernel(keep_ref, got_ref, far_ref, loss_ref, near1_ref, near2_ref):
    width = keep_ref.shape[1]
    far_loss = sum_lanes(far_ref[:16, width:], 0)
    lanes = (lanes3(loss_ref[:1, :1], 0, (32, 128)) + lanes3(far_loss, 3, (32, 128))).astype(BF16)
    near1_ref[:, width:] = lanes
    near2_ref[:, width:] = lanes
    near1 = keep_ref[32:64, :] + got_ref[:32, :].astype(F32) + far_ref[:32, :width].astype(F32)
    near1_ref[:, :width] = near1.astype(BF16)
    near2 = keep_ref[64:80, :] + got_ref[32:48, :].astype(F32) + far_ref[32:, :width].astype(F32)
    near2_ref[:16, :width] = near2.astype(BF16)
    near2_ref[16:, :width] = (keep_ref[80:96, :] + got_ref[48:64, :].astype(F32)).astype(BF16)


def line_kernel(b1, b2, loss_ref, rel_ref, line_ref):
    width = b1.shape[1] - 128
    rel = rel_ref[:1, :]
    line = jnp.where(rel == 0, loss_ref[:1, :1], 0.0)
    for step, ref, first in ((1, b1, 0), (3, b1, 3), (2, b2, 0), (4, b2, 3)):
        line = jnp.where(rel == step, sum_lanes(ref[:16, width:], first), line)
    line_ref[...] = jnp.broadcast_to(line[None], line_ref.shape)


def chip_sum_kernel(keep_ref, b1, b2, mine_ref, theirs_ref):
    rows, width = mine_ref.shape
    total = keep_ref[: 2 * rows, :] + b1[:, :width].astype(F32) + b2[:, :width].astype(F32)
    mine_ref[...] = total[:rows, :]
    theirs_ref[...] = total[rows:, :].astype(BF16)


def row_sum_kernel(own_ref, up, down, opposite, mine_ref, theirs_ref):
    total = own_ref[...] + up[...].astype(F32) + down[...].astype(F32)
    mine_ref[...] = total[:32, :] + opposite[...].astype(F32)
    theirs_ref[...] = total[32:, :].astype(BF16)


def finish_kernel(count):
    def kernel(mine_q, got_q, mine_p, got_p, line_ref, q_ref, p_ref, h_ref, loss_ref):
        rows = q_ref.shape[0]
        q_ref[...] = (mine_q[...] + got_q[...].astype(F32)).astype(BF16)
        total = mine_p[...] + got_p[...].astype(F32)
        p_ref[...] = total[:rows, :].astype(BF16)
        h_ref[...] = total[rows:, :].astype(BF16)
        line = jnp.sum(line_ref[...], axis=0)[:1, :]
        loss_ref[...] = jnp.sum(line, axis=1, keepdims=True) / count

    return kernel


def on_device(queries, passages, hard_passages, positive_ids, hard_ids):
    rows, width = queries.shape
    wide = width + 128
    batch = rows * NY * NX * NZ * 2
    per_query = hard_ids.shape[1]

    own_q, own_p = pl.pallas_call(
        own_kernel,
        out_shape=[pltpu.VMEM((rows, wide), BF16), pltpu.VMEM((2 * rows, width), BF16)],
        in_specs=[pl.BlockSpec(memory_space=pltpu.HBM)] * 5,
        out_specs=[pl.BlockSpec(memory_space=pltpu.VMEM)] * 2,
        scratch_shapes=[pltpu.VMEM((1, rows), I32), pltpu.VMEM((per_query, rows), I32), pltpu.SemaphoreType.DMA((5,))],
        compiler_params=pltpu.CompilerParams(vmem_limit_bytes=12 << 20),
    )(
        *(
            pltpu.with_memory_space_constraint(x, pltpu.HBM)
            for x in (queries, passages, hard_passages, positive_ids.reshape(1, rows), hard_ids.T)
        )
    )
    cols, rel = pl.pallas_call(
        place_kernel,
        out_shape=[pltpu.VMEM((8, 256), F32), pltpu.VMEM((8, 128), I32)],
        in_specs=[pl.BlockSpec(memory_space=pltpu.SMEM)],
        out_specs=[pl.BlockSpec(memory_space=pltpu.VMEM)] * 2,
    )(jnp.stack([lax.axis_index(name) for name in DP]))
    other_p = from_plane(own_p, (0, 1))
    (chip_q,) = call(pack_kernel, [((2 * rows, wide), BF16)], own_q, from_core(own_q))
    own_up, own_down = from_plane(own_p, (1, 0)), from_plane(own_p, (3, 0))
    other_up, other_down = from_plane(other_p, (1, 0)), from_plane(other_p, (3, 0))
    own_opposite = from_plane(own_p, (2, 0))
    other_opposite = from_plane(own_opposite, (0, 1))
    block_p = [own_p, other_p, own_up, other_up, own_opposite, other_opposite, own_down, other_down]
    near1, near2 = from_line(chip_q, 1), from_line(chip_q, 2)
    (far,) = call(far_kernel, [((48, wide), BF16)], near1, near2, after=[other_p])
    (both,) = call(pack_kernel, [((64, wide), BF16)], near1, near2, after=[cols, own_opposite, own_up, own_down])
    far = from_line(far, 2)
    far_parts = [from_core(x) for x in call(split_kernel, [((16, wide), BF16)] * 3, far)]

    scores, ids_all, q_all, p_all = call(
        scores_kernel,
        [((256, 256), F32), ((256, 128), BF16), ((256, width), BF16), ((256, width), BF16)],
        chip_q,
        near1,
        near2,
        far,
        from_core(both),
        *far_parts,
        *block_p,
    )
    other = lax.ppermute(scores, "pair", [(0, 1), (1, 0)])
    weights, loss = call(
        weights_kernel, [((256, 256), BF16), ((8, 128), F32)], scores, other, ids_all, cols
    )
    keep, send = call(
        grad_q_kernel, [((144, width), F32), ((128, width), BF16)], weights, p_all, loss
    )
    got = from_core(send)
    far, loss = call(far_sum_kernel, [((48, wide), BF16), ((8, 128), F32)], keep, got, loss)
    own, up, down, opposite, other = call(
        grad_p_kernel,
        [((64, width), F32), ((64, width), BF16), ((64, width), BF16), ((32, width), F32), ((32, width), BF16)],
        weights,
        q_all,
        after=[far],
    )
    (opposite,) = call(opposite_kernel, [((32, width), BF16)], opposite, from_plane(other, (0, 1)))
    parts = [from_plane(up, (3, 0)), from_plane(down, (1, 0)), from_plane(opposite, (2, 0))]
    far = from_line(far, 2, back=True)
    near1, near2 = call(near_sum_kernel, [((32, wide), BF16)] * 2, keep, got, far, loss)
    near1, near2 = from_line(near1, 1, back=True), from_line(near2, 2, back=True)
    mine_p, theirs_p = call(row_sum_kernel, [((32, width), F32), ((32, width), BF16)], own, *parts)
    (line,) = call(line_kernel, [((NY * NX * 2, LINE_ROWS, 128), F32)], near1, near2, loss, rel)
    mine, theirs = call(chip_sum_kernel, [((rows, width), F32), ((rows, width), BF16)], keep, near1, near2)
    line = lax.all_to_all(line, ("y", "xl", "core"), 0, 0, tiled=True)
    grad_q, grad_p, grad_h, mean_loss = call(
        finish_kernel(batch * (batch + per_query)),
        [((rows, width), BF16)] * 3 + [((1, 1), F32)],
        mine,
        from_core(theirs),
        mine_p,
        from_plane(theirs_p, (0, 1)),
        line,
        final=True,
    )
    return mean_loss.reshape(1), grad_q, grad_p, grad_h


def solution(mesh):
    spec = P(DP, "pair")
    return jax.shard_map(
        on_device,
        mesh=Mesh(mesh.devices.reshape(SHAPE), DP + ("pair",)),
        in_specs=(spec, spec, spec, P(DP), P(DP, None)),
        out_specs=(P(), spec, spec, spec),
        check_vma=False,
    )
```

```python
import math

import jax
import jax.numpy as jnp
from jax import lax
from jax.experimental import pallas as pl
from jax.experimental.pallas import tpu as pltpu
from jax.sharding import Mesh, PartitionSpec as P

D = 4096
SCALE = 1.0 / math.sqrt(D)
LOGIT_BIAS = -1.0
BF16, F32, I32 = jnp.bfloat16, jnp.float32, jnp.int32

SHAPE = (4, 2, 8, 2, 2)
DP = ("y", "xl", "z", "core")
PLANE = ("y", "xl")
LINE = ("z", "core")
NY, NX, NZ = 4, 2, 8
LINE_ROWS = 12


def call(kernel, outs, *args, scratch=(), after=(), final=False):
    count = len(args)

    def body(*refs):
        kernel(*refs[:count], *refs[count + len(after) :])

    return pl.pallas_call(
        body,
        out_shape=[jax.ShapeDtypeStruct(s, t) if final else pltpu.VMEM(s, t) for s, t in outs],
        in_specs=[pl.BlockSpec(memory_space=pltpu.VMEM)] * count + [pl.BlockSpec(memory_space=pl.ANY)] * len(after),
        out_specs=[pl.BlockSpec(memory_space=pltpu.VMEM) for _ in outs],
        scratch_shapes=[pltpu.VMEM(s, t) for s, t in scratch],
        compiler_params=pltpu.CompilerParams(vmem_limit_bytes=12 << 20),
    )(*args, *after)


def from_plane(x, step):
    dy, dx = step
    pairs = []
    for y in range(NY):
        for xl in range(NX):
            pairs.append((((y + dy) % NY) * NX + (xl + dx) % NX, y * NX + xl))
    return lax.ppermute(x, PLANE, pairs)


def from_line(x, step, back=False):
    pairs = []
    for z in range(NZ):
        for core in range(2):
            way = step if (core == 0) != back else -step
            pairs.append((((z + way) % NZ) * 2 + core, z * 2 + core))
    return lax.ppermute(x, LINE, pairs)


def from_core(x):
    return lax.ppermute(x, "core", [(0, 1), (1, 0)])


def pack(refs, scratch):
    at, width = 0, scratch.shape[1]
    for ref in refs:
        n = ref.shape[0]
        scratch[at : at + n, :] = ref[:, :width]
        at += n


def lanes3(x, first, shape):
    lane = lax.broadcasted_iota(I32, shape, 1)
    high = x.astype(BF16).astype(F32)
    mid = (x - high).astype(BF16).astype(F32)
    low = (x - high - mid).astype(BF16).astype(F32)
    out = jnp.zeros(shape, F32)
    for i, part in enumerate((high, mid, low)):
        out = jnp.where(lane == first + i, jnp.broadcast_to(part, shape), out)
    return out


def sum_lanes(x, first):
    lane = lax.broadcasted_iota(I32, (1, 128), 1)
    return jnp.sum(jnp.where((lane >= first) & (lane < first + 3), x[:1, :].astype(F32), 0.0), axis=1, keepdims=True)


def own_kernel(q_ref, p_ref, h_ref, pos_ref, hard_ref, own_q, own_p, pos, hard, sems):
    rows, width = q_ref.shape
    moves = [
        (pos_ref, pos),
        (hard_ref, hard),
        (q_ref, own_q.at[:, :width]),
        (p_ref, own_p.at[:rows, :]),
        (h_ref, own_p.at[rows:, :]),
    ]
    copies = [pltpu.make_async_copy(src, dst, sems.at[i]) for i, (src, dst) in enumerate(moves)]
    for copy in copies:
        copy.start()
    copies[0].wait()
    copies[1].wait()
    lane = lax.broadcasted_iota(I32, (8, 128), 1)
    row = lax.broadcasted_iota(I32, (8, 128), 0)
    ids = jnp.zeros((rows, 128), F32)
    first = jnp.broadcast_to(pos[...], (8, rows))
    for shift, part in ((0, lambda v: v >> 4), (16, lambda v: v & 15)):
        for values, at in ((hard[...], lane == row + 1 + shift), (first, (lane == shift) & (row == 0))):
            ids = ids + lax.dot_general(
                part(values).astype(F32).astype(BF16),
                jnp.where(at, 1.0, 0.0).astype(BF16),
                (((0,), (0,)), ((), ())),
                preferred_element_type=F32,
            )
    own_q[:, width:] = ids.astype(BF16)
    for copy in copies[2:]:
        copy.wait()


def place_kernel(at_ref, cols_ref, rel_ref):
    lane = lax.broadcasted_iota(I32, (8, 128), 1)
    y = (at_ref[0] + (lane >> 5)) & (NY - 1)
    x = (at_ref[1] + (lane >> 4)) & (NX - 1)
    line = at_ref[2] * 2 + at_ref[3]
    row = lax.broadcasted_iota(I32, (8, 128), 0)
    cols_ref[...] = jnp.where(row == 0, ((y * NX + x) * (NZ * 2) + line) * 16 + (lane & 15), line).astype(F32)
    lane = lax.broadcasted_iota(I32, (8, 128), 1)
    rel = jnp.where(at_ref[3] == 0, at_ref[2] - lane, lane - at_ref[2]) & (NZ - 1)
    rel_ref[...] = jnp.where((lane >= NZ) | ((at_ref[3] == 1) & ((rel & 3) == 0)), NZ, rel)


def pack_kernel(*refs):
    pack(refs[:-1], refs[-1])


def split_kernel(ref, *parts):
    for i, part in enumerate(parts):
        part[...] = ref[16 * i : 16 * i + 16, :]


def far_kernel(near1, near2, far):
    far[:32, :] = near1[...]
    far[32:, :] = near2[:16, :]


def id_columns(ids_ref):
    ids = ids_ref[...].astype(F32)
    return ids[:, :16] * 16.0 + ids[:, 16:32], ids[:, :16]


def fold(columns, shape):
    lane, row = lax.broadcasted_iota(I32, shape, 1), lax.broadcasted_iota(I32, shape, 0)
    wide = jnp.zeros(shape, F32)
    for k, column in enumerate(columns):
        wide = jnp.where((lane & 7) == k, column, wide)
    wide = jnp.where((lane >> 3) == (row >> 4), wide, 0.0)
    total = wide[:16, :]
    for g in range(1, 16):
        total = total + wide[16 * g : 16 * g + 16, :]
    return total


def scores_kernel(*refs):
    q_refs, p_refs, cols_ref, (s_ref, ids_ref, q_all, p_all) = refs[:8], refs[8:16], refs[16], refs[17:]
    width = p_all.shape[1]
    pack(q_refs, q_all)
    for k, ref in enumerate(p_refs):
        p_all[16 * k : 16 * k + 16, :] = ref[:16, :]
        p_all[128 + 16 * k : 144 + 16 * k, :] = ref[16:, :]
    at = 0
    for ref in q_refs:
        n = ref.shape[0]
        ids_ref[at : at + n, :] = ref[:, width:]
        at += n
    scores = lax.dot_general(q_all[...], p_all[...], (((1,), (1,)), ((), ())), preferred_element_type=F32)
    s_ref[:256, :] = scores[:, :128]
    hard = scores[:, 128:]
    col = jnp.broadcast_to(cols_ref[:1, :], hard.shape)
    ids, _ = id_columns(ids_ref)
    picked = [
        jnp.sum(jnp.where(ids[:, k : k + 1] == col, hard, 0.0), axis=1, keepdims=True) for k in range(1, 9)
    ]
    s_ref[256:, :] = fold(picked, hard.shape)


def sigmoid_softplus(logits):
    e = jnp.exp(-jnp.abs(logits))
    return jnp.where(logits >= 0.0, 1.0, e) / (1.0 + e), jnp.maximum(logits, 0.0) + jnp.log1p(e)


def sum_all(x):
    return jnp.sum(jnp.sum(x, axis=1, keepdims=True), axis=0, keepdims=True)


def weights_kernel(s_ref, got_ref, ids_ref, cols_ref, w_ref, loss_ref):
    logits = SCALE * (s_ref[...] + got_ref[...]) + LOGIT_BIAS
    sigmoid, softplus = sigmoid_softplus(logits)
    ids, owners = id_columns(ids_ref)
    shape = (256, 128)
    col = jnp.broadcast_to(cols_ref[:1, :], shape)
    labels = (ids[:, :1] == col).astype(F32)
    w_ref[:, :128] = ((sigmoid[:256, :] - labels) * SCALE).astype(BF16)
    loss = sum_all(softplus[:256, :] - labels * logits[:256, :])

    line = cols_ref[1:2, :1].astype(I32)
    here = ((owners.astype(I32) & 15) == line).astype(F32)
    here = fold([here[:, k : k + 1] for k in range(1, 9)], shape)
    loss = loss + sum_all(jnp.where(here > 0.0, softplus[256:, :], 0.0))
    loss_ref[...] = jnp.broadcast_to(loss, loss_ref.shape)
    hard = (sigmoid[256:, :] * SCALE).astype(BF16).astype(F32)
    lane, row = lax.broadcasted_iota(I32, shape, 1), lax.broadcasted_iota(I32, shape, 0)
    hard = jnp.where((lane >> 3) == (row >> 4), jnp.concatenate([hard] * 16, axis=0), 0.0).astype(BF16)
    lane, row = lax.broadcasted_iota(I32, (128, 128), 1), lax.broadcasted_iota(I32, (128, 128), 0)
    unfold = jnp.where((row & 7) == lane, 1.0, 0.0).astype(BF16)
    hard = jnp.dot(hard, unfold, preferred_element_type=F32)
    total = jnp.zeros(shape, F32)
    for k in range(8):
        total = total + jnp.where(ids[:, k + 1 : k + 2] == col, hard[:, k : k + 1], 0.0)
    w_ref[:, 128:] = total.astype(BF16)


def grad_q_kernel(w_ref, p_all, loss_ref, keep_ref, send_ref):
    part = jnp.dot(w_ref[...], p_all[...], preferred_element_type=F32)
    keep_ref[...] = part[:144, :]
    send_ref[:112, :] = part[144:, :].astype(BF16)
    send_ref[112:, :128] = lanes3(loss_ref[:1, :1], 0, (16, 128)).astype(BF16)
    send_ref[112:, 128:] = jnp.zeros((16, send_ref.shape[1] - 128), BF16)


def grad_p_kernel(w_ref, q_all, own_ref, up_ref, down_ref, opposite_ref, other_ref):
    part = lax.dot_general(w_ref[...], q_all[...], (((0,), (0,)), ((), ())), preferred_element_type=F32)
    places = [(own_ref, 0), (own_ref, 32), (up_ref, 0), (up_ref, 32), (opposite_ref, 0), (other_ref, 0), (down_ref, 0)]
    for k, (ref, at) in enumerate(places + [(down_ref, 32)]):
        ref[at : at + 16, :] = part[16 * k : 16 * k + 16, :].astype(ref.dtype)
        ref[at + 16 : at + 32, :] = part[128 + 16 * k : 144 + 16 * k, :].astype(ref.dtype)


def opposite_kernel(mine_ref, got_ref, out_ref):
    out_ref[...] = (mine_ref[...] + got_ref[...].astype(F32)).astype(BF16)


def far_sum_kernel(keep_ref, got_ref, loss_ref, far_ref, chip_loss_ref):
    width = keep_ref.shape[1]
    loss = loss_ref[:1, :1] + sum_lanes(got_ref[112:, :128], 0)
    chip_loss_ref[...] = jnp.broadcast_to(loss, chip_loss_ref.shape)
    far_ref[:, :width] = (keep_ref[96:144, :] + got_ref[64:112, :].astype(F32)).astype(BF16)
    far_ref[:, width:] = lanes3(loss, 0, (48, 128)).astype(BF16)


def near_sum_kernel(keep_ref, got_ref, far_ref, loss_ref, near1_ref, near2_ref):
    width = keep_ref.shape[1]
    far_loss = sum_lanes(far_ref[:16, width:], 0)
    lanes = (lanes3(loss_ref[:1, :1], 0, (32, 128)) + lanes3(far_loss, 3, (32, 128))).astype(BF16)
    near1_ref[:, width:] = lanes
    near2_ref[:, width:] = lanes
    near1 = keep_ref[32:64, :] + got_ref[:32, :].astype(F32) + far_ref[:32, :width].astype(F32)
    near1_ref[:, :width] = near1.astype(BF16)
    near2 = keep_ref[64:80, :] + got_ref[32:48, :].astype(F32) + far_ref[32:, :width].astype(F32)
    near2_ref[:16, :width] = near2.astype(BF16)
    near2_ref[16:, :width] = (keep_ref[80:96, :] + got_ref[48:64, :].astype(F32)).astype(BF16)


def line_kernel(b1, b2, loss_ref, rel_ref, line_ref):
    width = b1.shape[1] - 128
    rel = rel_ref[:1, :]
    line = jnp.where(rel == 0, loss_ref[:1, :1], 0.0)
    for step, ref, first in ((1, b1, 0), (3, b1, 3), (2, b2, 0), (4, b2, 3)):
        line = jnp.where(rel == step, sum_lanes(ref[:16, width:], first), line)
    line_ref[...] = jnp.broadcast_to(line[None], line_ref.shape)


def chip_sum_kernel(keep_ref, b1, b2, mine_ref, theirs_ref):
    rows, width = mine_ref.shape
    total = keep_ref[: 2 * rows, :] + b1[:, :width].astype(F32) + b2[:, :width].astype(F32)
    mine_ref[...] = total[:rows, :]
    theirs_ref[...] = total[rows:, :].astype(BF16)


def row_sum_kernel(own_ref, up, down, opposite, mine_ref, theirs_ref):
    total = own_ref[...] + up[...].astype(F32) + down[...].astype(F32)
    mine_ref[...] = total[:32, :] + opposite[...].astype(F32)
    theirs_ref[...] = total[32:, :].astype(BF16)


def finish_kernel(count):
    def kernel(mine_q, got_q, mine_p, got_p, line_ref, q_ref, p_ref, h_ref, loss_ref):
        rows = q_ref.shape[0]
        q_ref[...] = (mine_q[...] + got_q[...].astype(F32)).astype(BF16)
        total = mine_p[...] + got_p[...].astype(F32)
        p_ref[...] = total[:rows, :].astype(BF16)
        h_ref[...] = total[rows:, :].astype(BF16)
        line = jnp.sum(line_ref[...], axis=0)[:1, :]
        loss_ref[...] = jnp.sum(line, axis=1, keepdims=True) / count

    return kernel


def on_device(queries, passages, hard_passages, positive_ids, hard_ids):
    rows, width = queries.shape
    wide = width + 128
    batch = rows * NY * NX * NZ * 2
    per_query = hard_ids.shape[1]

    own_q, own_p = pl.pallas_call(
        own_kernel,
        out_shape=[pltpu.VMEM((rows, wide), BF16), pltpu.VMEM((2 * rows, width), BF16)],
        in_specs=[pl.BlockSpec(memory_space=pltpu.HBM)] * 5,
        out_specs=[pl.BlockSpec(memory_space=pltpu.VMEM)] * 2,
        scratch_shapes=[pltpu.VMEM((1, rows), I32), pltpu.VMEM((per_query, rows), I32), pltpu.SemaphoreType.DMA((5,))],
        compiler_params=pltpu.CompilerParams(vmem_limit_bytes=12 << 20),
    )(
        *(
            pltpu.with_memory_space_constraint(x, pltpu.HBM)
            for x in (queries, passages, hard_passages, positive_ids.reshape(1, rows), hard_ids.T)
        )
    )
    cols, rel = pl.pallas_call(
        place_kernel,
        out_shape=[pltpu.VMEM((8, 128), F32), pltpu.VMEM((8, 128), I32)],
        in_specs=[pl.BlockSpec(memory_space=pltpu.SMEM)],
        out_specs=[pl.BlockSpec(memory_space=pltpu.VMEM)] * 2,
    )(jnp.stack([lax.axis_index(name) for name in DP]))
    other_p = from_plane(own_p, (0, 1))
    (chip_q,) = call(pack_kernel, [((2 * rows, wide), BF16)], own_q, from_core(own_q))
    own_up, own_down = from_plane(own_p, (1, 0)), from_plane(own_p, (3, 0))
    other_up, other_down = from_plane(other_p, (1, 0)), from_plane(other_p, (3, 0))
    own_opposite = from_plane(own_p, (2, 0))
    other_opposite = from_plane(own_opposite, (0, 1))
    block_p = [own_p, other_p, own_up, other_up, own_opposite, other_opposite, own_down, other_down]
    near1, near2 = from_line(chip_q, 1), from_line(chip_q, 2)
    (far,) = call(far_kernel, [((48, wide), BF16)], near1, near2, after=[other_p])
    (both,) = call(pack_kernel, [((64, wide), BF16)], near1, near2, after=[cols, own_opposite, own_up, own_down])
    far = from_line(far, 2)
    far_parts = [from_core(x) for x in call(split_kernel, [((16, wide), BF16)] * 3, far)]

    scores, ids_all, q_all, p_all = call(
        scores_kernel,
        [((272, 128), F32), ((256, 128), BF16), ((256, width), BF16), ((256, width), BF16)],
        chip_q,
        near1,
        near2,
        far,
        from_core(both),
        *far_parts,
        *block_p,
        cols,
    )
    other = lax.ppermute(scores, "pair", [(0, 1), (1, 0)])
    weights, loss = call(
        weights_kernel, [((256, 256), BF16), ((8, 128), F32)], scores, other, ids_all, cols
    )
    keep, send = call(
        grad_q_kernel, [((144, width), F32), ((128, width), BF16)], weights, p_all, loss
    )
    got = from_core(send)
    far, loss = call(far_sum_kernel, [((48, wide), BF16), ((8, 128), F32)], keep, got, loss)
    own, up, down, opposite, other = call(
        grad_p_kernel,
        [((64, width), F32), ((64, width), BF16), ((64, width), BF16), ((32, width), F32), ((32, width), BF16)],
        weights,
        q_all,
        after=[far],
    )
    (opposite,) = call(opposite_kernel, [((32, width), BF16)], opposite, from_plane(other, (0, 1)))
    parts = [from_plane(up, (3, 0)), from_plane(down, (1, 0)), from_plane(opposite, (2, 0))]
    far = from_line(far, 2, back=True)
    near1, near2 = call(near_sum_kernel, [((32, wide), BF16)] * 2, keep, got, far, loss)
    near1, near2 = from_line(near1, 1, back=True), from_line(near2, 2, back=True)
    mine_p, theirs_p = call(row_sum_kernel, [((32, width), F32), ((32, width), BF16)], own, *parts)
    (line,) = call(line_kernel, [((NY * NX * 2, LINE_ROWS, 128), F32)], near1, near2, loss, rel)
    mine, theirs = call(chip_sum_kernel, [((rows, width), F32), ((rows, width), BF16)], keep, near1, near2)
    line = lax.all_to_all(line, ("y", "xl", "core"), 0, 0, tiled=True)
    grad_q, grad_p, grad_h, mean_loss = call(
        finish_kernel(batch * (batch + per_query)),
        [((rows, width), BF16)] * 3 + [((1, 1), F32)],
        mine,
        from_core(theirs),
        mine_p,
        from_plane(theirs_p, (0, 1)),
        line,
        final=True,
    )
    return mean_loss.reshape(1), grad_q, grad_p, grad_h


def solution(mesh):
    spec = P(DP, "pair")
    return jax.shard_map(
        on_device,
        mesh=Mesh(mesh.devices.reshape(SHAPE), DP + ("pair",)),
        in_specs=(spec, spec, spec, P(DP), P(DP, None)),
        out_specs=(P(), spec, spec, spec),
        check_vma=False,
    )
```

```python
import math

import jax
import jax.numpy as jnp
from jax import lax
from jax.experimental import pallas as pl
from jax.experimental.pallas import tpu as pltpu
from jax.sharding import Mesh, PartitionSpec as P

D = 4096
SCALE = 1.0 / math.sqrt(D)
LOGIT_BIAS = -1.0
BF16, F32, I32 = jnp.bfloat16, jnp.float32, jnp.int32

SHAPE = (4, 2, 8, 2, 2)
DP = ("y", "xl", "z", "core")
PLANE = ("y", "xl")
LINE = ("z", "core")
NY, NX, NZ = 4, 2, 8
LINE_ROWS = 12


def call(kernel, outs, *args, scratch=(), after=(), final=False):
    count = len(args)

    def body(*refs):
        kernel(*refs[:count], *refs[count + len(after) :])

    return pl.pallas_call(
        body,
        out_shape=[jax.ShapeDtypeStruct(s, t) if final else pltpu.VMEM(s, t) for s, t in outs],
        in_specs=[pl.BlockSpec(memory_space=pltpu.VMEM)] * count + [pl.BlockSpec(memory_space=pl.ANY)] * len(after),
        out_specs=[pl.BlockSpec(memory_space=pltpu.VMEM) for _ in outs],
        scratch_shapes=[pltpu.VMEM(s, t) for s, t in scratch],
        compiler_params=pltpu.CompilerParams(vmem_limit_bytes=12 << 20),
    )(*args, *after)


def from_plane(x, step):
    dy, dx = step
    pairs = []
    for y in range(NY):
        for xl in range(NX):
            pairs.append((((y + dy) % NY) * NX + (xl + dx) % NX, y * NX + xl))
    return lax.ppermute(x, PLANE, pairs)


def from_line(x, step, back=False):
    pairs = []
    for z in range(NZ):
        for core in range(2):
            way = step if (core == 0) != back else -step
            pairs.append((((z + way) % NZ) * 2 + core, z * 2 + core))
    return lax.ppermute(x, LINE, pairs)


def from_core(x):
    return lax.ppermute(x, "core", [(0, 1), (1, 0)])


def pack(refs, scratch):
    at, width = 0, scratch.shape[1]
    for ref in refs:
        n = ref.shape[0]
        scratch[at : at + n, :] = ref[:, :width]
        at += n


def lanes3(x, first, shape):
    lane = lax.broadcasted_iota(I32, shape, 1)
    high = x.astype(BF16).astype(F32)
    mid = (x - high).astype(BF16).astype(F32)
    low = (x - high - mid).astype(BF16).astype(F32)
    out = jnp.zeros(shape, F32)
    for i, part in enumerate((high, mid, low)):
        out = jnp.where(lane == first + i, jnp.broadcast_to(part, shape), out)
    return out


def sum_lanes(x, first):
    lane = lax.broadcasted_iota(I32, (1, 128), 1)
    return jnp.sum(jnp.where((lane >= first) & (lane < first + 3), x[:1, :].astype(F32), 0.0), axis=1, keepdims=True)


def own_kernel(q_ref, p_ref, h_ref, pos_ref, hard_ref, own_q, own_p, pos, hard, sems):
    rows, width = q_ref.shape
    moves = [
        (pos_ref, pos),
        (hard_ref, hard),
        (q_ref, own_q.at[:, :width]),
        (p_ref, own_p.at[:rows, :]),
        (h_ref, own_p.at[rows:, :]),
    ]
    copies = [pltpu.make_async_copy(src, dst, sems.at[i]) for i, (src, dst) in enumerate(moves)]
    for copy in copies:
        copy.start()
    copies[0].wait()
    copies[1].wait()
    lane = lax.broadcasted_iota(I32, (8, 128), 1)
    row = lax.broadcasted_iota(I32, (8, 128), 0)
    ids = jnp.zeros((rows, 128), F32)
    first = jnp.broadcast_to(pos[...], (8, rows))
    for shift, part in ((0, lambda v: v >> 4), (16, lambda v: v & 15)):
        for values, at in ((hard[...], lane == row + 1 + shift), (first, (lane == shift) & (row == 0))):
            ids = ids + lax.dot_general(
                part(values).astype(F32).astype(BF16),
                jnp.where(at, 1.0, 0.0).astype(BF16),
                (((0,), (0,)), ((), ())),
                preferred_element_type=F32,
            )
    own_q[:, width:] = ids.astype(BF16)
    for copy in copies[2:]:
        copy.wait()


def place_kernel(at_ref, cols_ref, rel_ref, pool_ref):
    lane = lax.broadcasted_iota(I32, (8, 128), 1)
    y = (at_ref[0] + (lane >> 5)) & (NY - 1)
    x = (at_ref[1] + (lane >> 4)) & (NX - 1)
    line = at_ref[2] * 2 + at_ref[3]
    row = lax.broadcasted_iota(I32, (8, 128), 0)
    cols_ref[...] = jnp.where(row == 0, ((y * NX + x) * (NZ * 2) + line) * 16 + (lane & 15), line).astype(F32)
    row = lax.broadcasted_iota(I32, pool_ref.shape, 0)
    y, x = (at_ref[0] + (row >> 5)) & (NY - 1), (at_ref[1] + (row >> 4)) & (NX - 1)
    pool_ref[...] = (((y * NX + x) * (NZ * 2) + line) * 16 + (row & 15)).astype(F32)
    lane = lax.broadcasted_iota(I32, (8, 128), 1)
    rel = jnp.where(at_ref[3] == 0, at_ref[2] - lane, lane - at_ref[2]) & (NZ - 1)
    rel_ref[...] = jnp.where((lane >= NZ) | ((at_ref[3] == 1) & ((rel & 3) == 0)), NZ, rel)


def pack_kernel(*refs):
    pack(refs[:-1], refs[-1])


def split_kernel(ref, *parts):
    for i, part in enumerate(parts):
        part[...] = ref[16 * i : 16 * i + 16, :]


def far_kernel(near1, near2, far):
    far[:32, :] = near1[...]
    far[32:, :] = near2[:16, :]


def id_row(ids_ref, k):
    return ids_ref[k : k + 1, :] * 16.0 + ids_ref[16 + k : 17 + k, :]


def scores_kernel(*refs):
    q_refs, p_refs, pool_ref, (s_ref, pos_ref, ids_ref, q_all, p_all, ids_all) = refs[:8], refs[8:16], refs[16], refs[17:]
    width = p_all.shape[1]
    pack(q_refs, q_all)
    for k, ref in enumerate(p_refs):
        p_all[16 * k : 16 * k + 16, :] = ref[:16, :]
        p_all[128 + 16 * k : 144 + 16 * k, :] = ref[16:, :]
    at = 0
    for ref in q_refs:
        n = ref.shape[0]
        ids_all[at : at + n, :] = ref[:, width:]
        at += n
    across = (((1,), (1,)), ((), ()))
    s_ref[:256, :] = lax.dot_general(q_all[...], p_all[:128, :], across, preferred_element_type=F32)
    ids = ids_all[...].astype(F32)
    pos_ref[...] = jnp.broadcast_to(ids[:, :1] * 16.0 + ids[:, 16:17], pos_ref.shape)
    lane, row = lax.broadcasted_iota(I32, (128, 128), 1), lax.broadcasted_iota(I32, (128, 128), 0)
    turn = jnp.where(lane == row, 1.0, 0.0).astype(BF16)
    ids_ref[...] = lax.dot_general(turn, ids_all[...], across, preferred_element_type=F32)[:32, :]
    hard = lax.dot_general(p_all[128:, :], q_all[...], across, preferred_element_type=F32)
    for k in range(8):
        mine = jnp.where(pool_ref[...] == id_row(ids_ref, k + 1), hard, 0.0)
        picked = jnp.sum(mine, axis=0, keepdims=True)
        s_ref[256 + k : 257 + k, :] = picked[:, :128]
        s_ref[264 + k : 265 + k, :] = picked[:, 128:]


def sigmoid_softplus(logits):
    e = jnp.exp(-jnp.abs(logits))
    return jnp.where(logits >= 0.0, 1.0, e) / (1.0 + e), jnp.maximum(logits, 0.0) + jnp.log1p(e)


def sum_all(x):
    return jnp.sum(jnp.sum(x, axis=1, keepdims=True), axis=0, keepdims=True)


def weights_kernel(s_ref, got_ref, pos_ref, ids_ref, cols_ref, pool_ref, w_ref, hard_ref, loss_ref):
    logits = SCALE * (s_ref[...] + got_ref[...]) + LOGIT_BIAS
    sigmoid, softplus = sigmoid_softplus(logits)
    labels = (pos_ref[...] == cols_ref[:1, :]).astype(F32)
    w_ref[...] = ((sigmoid[:256, :] - labels) * SCALE).astype(BF16)
    loss = sum_all(softplus[:256, :] - labels * logits[:256, :])

    line = cols_ref[1:2, :1].astype(I32)
    here = (ids_ref[1:9, :].astype(I32) & 15) == line
    hard, cost = (jnp.concatenate([x[256:264, :], x[264:, :]], axis=1) for x in (sigmoid, softplus))
    loss = loss + sum_all(jnp.where(here, cost, 0.0))
    loss_ref[...] = jnp.broadcast_to(loss, loss_ref.shape)
    hard = (hard * SCALE).astype(BF16).astype(F32)
    total = jnp.zeros(pool_ref.shape, F32)
    for k in range(8):
        total = total + jnp.where(pool_ref[...] == id_row(ids_ref, k + 1), hard[k : k + 1, :], 0.0)
    hard_ref[...] = total.astype(BF16)


def grad_q_kernel(w_ref, hard_ref, p_all, loss_ref, keep_ref, send_ref):
    part = jnp.dot(w_ref[...], p_all[:128, :], preferred_element_type=F32)
    part = part + lax.dot_general(
        hard_ref[...], p_all[128:, :], (((0,), (0,)), ((), ())), preferred_element_type=F32
    )
    keep_ref[...] = part[:144, :]
    send_ref[:112, :] = part[144:, :].astype(BF16)
    send_ref[112:, :128] = lanes3(loss_ref[:1, :1], 0, (16, 128)).astype(BF16)
    send_ref[112:, 128:] = jnp.zeros((16, send_ref.shape[1] - 128), BF16)


def grad_p_kernel(w_ref, hard_ref, q_all, own_ref, up_ref, down_ref, opposite_ref, other_ref):
    part = lax.dot_general(w_ref[...], q_all[...], (((0,), (0,)), ((), ())), preferred_element_type=F32)
    hard = jnp.dot(hard_ref[...], q_all[...], preferred_element_type=F32)
    places = [(own_ref, 0), (own_ref, 32), (up_ref, 0), (up_ref, 32), (opposite_ref, 0), (other_ref, 0), (down_ref, 0)]
    for k, (ref, at) in enumerate(places + [(down_ref, 32)]):
        ref[at : at + 16, :] = part[16 * k : 16 * k + 16, :].astype(ref.dtype)
        ref[at + 16 : at + 32, :] = hard[16 * k : 16 * k + 16, :].astype(ref.dtype)


def opposite_kernel(mine_ref, got_ref, out_ref):
    out_ref[...] = (mine_ref[...] + got_ref[...].astype(F32)).astype(BF16)


def far_sum_kernel(keep_ref, got_ref, loss_ref, far_ref, chip_loss_ref):
    width = keep_ref.shape[1]
    loss = loss_ref[:1, :1] + sum_lanes(got_ref[112:, :128], 0)
    chip_loss_ref[...] = jnp.broadcast_to(loss, chip_loss_ref.shape)
    far_ref[:, :width] = (keep_ref[96:144, :] + got_ref[64:112, :].astype(F32)).astype(BF16)
    far_ref[:, width:] = lanes3(loss, 0, (48, 128)).astype(BF16)


def near_sum_kernel(keep_ref, got_ref, far_ref, loss_ref, near1_ref, near2_ref):
    width = keep_ref.shape[1]
    far_loss = sum_lanes(far_ref[:16, width:], 0)
    lanes = (lanes3(loss_ref[:1, :1], 0, (32, 128)) + lanes3(far_loss, 3, (32, 128))).astype(BF16)
    near1_ref[:, width:] = lanes
    near2_ref[:, width:] = lanes
    near1 = keep_ref[32:64, :] + got_ref[:32, :].astype(F32) + far_ref[:32, :width].astype(F32)
    near1_ref[:, :width] = near1.astype(BF16)
    near2 = keep_ref[64:80, :] + got_ref[32:48, :].astype(F32) + far_ref[32:, :width].astype(F32)
    near2_ref[:16, :width] = near2.astype(BF16)
    near2_ref[16:, :width] = (keep_ref[80:96, :] + got_ref[48:64, :].astype(F32)).astype(BF16)


def line_kernel(b1, b2, loss_ref, rel_ref, line_ref):
    width = b1.shape[1] - 128
    rel = rel_ref[:1, :]
    line = jnp.where(rel == 0, loss_ref[:1, :1], 0.0)
    for step, ref, first in ((1, b1, 0), (3, b1, 3), (2, b2, 0), (4, b2, 3)):
        line = jnp.where(rel == step, sum_lanes(ref[:16, width:], first), line)
    line_ref[...] = jnp.broadcast_to(line[None], line_ref.shape)


def chip_sum_kernel(keep_ref, b1, b2, mine_ref, theirs_ref):
    rows, width = mine_ref.shape
    total = keep_ref[: 2 * rows, :] + b1[:, :width].astype(F32) + b2[:, :width].astype(F32)
    mine_ref[...] = total[:rows, :]
    theirs_ref[...] = total[rows:, :].astype(BF16)


def row_sum_kernel(own_ref, up, down, opposite, mine_ref, theirs_ref):
    total = own_ref[...] + up[...].astype(F32) + down[...].astype(F32)
    mine_ref[...] = total[:32, :] + opposite[...].astype(F32)
    theirs_ref[...] = total[32:, :].astype(BF16)


def finish_kernel(count):
    def kernel(mine_q, got_q, mine_p, got_p, line_ref, q_ref, p_ref, h_ref, loss_ref):
        rows = q_ref.shape[0]
        q_ref[...] = (mine_q[...] + got_q[...].astype(F32)).astype(BF16)
        total = mine_p[...] + got_p[...].astype(F32)
        p_ref[...] = total[:rows, :].astype(BF16)
        h_ref[...] = total[rows:, :].astype(BF16)
        line = jnp.sum(line_ref[...], axis=0)[:1, :]
        loss_ref[...] = jnp.sum(line, axis=1, keepdims=True) / count

    return kernel


def on_device(queries, passages, hard_passages, positive_ids, hard_ids):
    rows, width = queries.shape
    wide = width + 128
    batch = rows * NY * NX * NZ * 2
    per_query = hard_ids.shape[1]

    own_q, own_p = pl.pallas_call(
        own_kernel,
        out_shape=[pltpu.VMEM((rows, wide), BF16), pltpu.VMEM((2 * rows, width), BF16)],
        in_specs=[pl.BlockSpec(memory_space=pltpu.HBM)] * 5,
        out_specs=[pl.BlockSpec(memory_space=pltpu.VMEM)] * 2,
        scratch_shapes=[pltpu.VMEM((1, rows), I32), pltpu.VMEM((per_query, rows), I32), pltpu.SemaphoreType.DMA((5,))],
        compiler_params=pltpu.CompilerParams(vmem_limit_bytes=12 << 20),
    )(
        *(
            pltpu.with_memory_space_constraint(x, pltpu.HBM)
            for x in (queries, passages, hard_passages, positive_ids.reshape(1, rows), hard_ids.T)
        )
    )
    cols, rel, pool = pl.pallas_call(
        place_kernel,
        out_shape=[pltpu.VMEM((8, 128), F32), pltpu.VMEM((8, 128), I32), pltpu.VMEM((128, 256), F32)],
        in_specs=[pl.BlockSpec(memory_space=pltpu.SMEM)],
        out_specs=[pl.BlockSpec(memory_space=pltpu.VMEM)] * 3,
    )(jnp.stack([lax.axis_index(name) for name in DP]))
    other_p = from_plane(own_p, (0, 1))
    (chip_q,) = call(pack_kernel, [((2 * rows, wide), BF16)], own_q, from_core(own_q))
    own_up, own_down = from_plane(own_p, (1, 0)), from_plane(own_p, (3, 0))
    other_up, other_down = from_plane(other_p, (1, 0)), from_plane(other_p, (3, 0))
    own_opposite = from_plane(own_p, (2, 0))
    other_opposite = from_plane(own_opposite, (0, 1))
    block_p = [own_p, other_p, own_up, other_up, own_opposite, other_opposite, own_down, other_down]
    near1, near2 = from_line(chip_q, 1), from_line(chip_q, 2)
    (far,) = call(far_kernel, [((48, wide), BF16)], near1, near2, after=[other_p])
    (both,) = call(pack_kernel, [((64, wide), BF16)], near1, near2, after=[cols, own_opposite, own_up, own_down])
    far = from_line(far, 2)
    far_parts = [from_core(x) for x in call(split_kernel, [((16, wide), BF16)] * 3, far)]

    scores, pos, ids, q_all, p_all = call(
        scores_kernel,
        [
            ((272, 128), F32),
            ((256, 128), F32),
            ((32, 256), F32),
            ((256, width), BF16),
            ((256, width), BF16),
        ],
        chip_q,
        near1,
        near2,
        far,
        from_core(both),
        *far_parts,
        *block_p,
        pool,
        scratch=[((256, 128), BF16)],
    )
    other = lax.ppermute(scores, "pair", [(0, 1), (1, 0)])
    weights, hard, loss = call(
        weights_kernel,
        [((256, 128), BF16), ((128, 256), BF16), ((8, 128), F32)],
        scores,
        other,
        pos,
        ids,
        cols,
        pool,
    )
    keep, send = call(
        grad_q_kernel, [((144, width), F32), ((128, width), BF16)], weights, hard, p_all, loss
    )
    got = from_core(send)
    own, up, down, opposite, other = call(
        grad_p_kernel,
        [((64, width), F32), ((64, width), BF16), ((64, width), BF16), ((32, width), F32), ((32, width), BF16)],
        weights,
        hard,
        q_all,
    )
    far, loss = call(far_sum_kernel, [((48, wide), BF16), ((8, 128), F32)], keep, got, loss, after=[own])
    (opposite,) = call(opposite_kernel, [((32, width), BF16)], opposite, from_plane(other, (0, 1)))
    parts = [from_plane(up, (3, 0)), from_plane(down, (1, 0)), from_plane(opposite, (2, 0))]
    far = from_line(far, 2, back=True)
    near1, near2 = call(near_sum_kernel, [((32, wide), BF16)] * 2, keep, got, far, loss)
    near1, near2 = from_line(near1, 1, back=True), from_line(near2, 2, back=True)
    mine_p, theirs_p = call(row_sum_kernel, [((32, width), F32), ((32, width), BF16)], own, *parts)
    (line,) = call(line_kernel, [((NY * NX * 2, LINE_ROWS, 128), F32)], near1, near2, loss, rel)
    mine, theirs = call(chip_sum_kernel, [((rows, width), F32), ((rows, width), BF16)], keep, near1, near2)
    line = lax.all_to_all(line, ("y", "xl", "core"), 0, 0, tiled=True)
    grad_q, grad_p, grad_h, mean_loss = call(
        finish_kernel(batch * (batch + per_query)),
        [((rows, width), BF16)] * 3 + [((1, 1), F32)],
        mine,
        from_core(theirs),
        mine_p,
        from_plane(theirs_p, (0, 1)),
        line,
        final=True,
    )
    return mean_loss.reshape(1), grad_q, grad_p, grad_h


def solution(mesh):
    spec = P(DP, "pair")
    return jax.shard_map(
        on_device,
        mesh=Mesh(mesh.devices.reshape(SHAPE), DP + ("pair",)),
        in_specs=(spec, spec, spec, P(DP), P(DP, None)),
        out_specs=(P(), spec, spec, spec),
        check_vma=False,
    )
```

```python
import math

import jax
import jax.numpy as jnp
from jax import lax
from jax.experimental import pallas as pl
from jax.experimental.pallas import tpu as pltpu
from jax.sharding import Mesh, PartitionSpec as P

D = 4096
SCALE = 1.0 / math.sqrt(D)
LOGIT_BIAS = -1.0
BF16, F32, I32 = jnp.bfloat16, jnp.float32, jnp.int32

SHAPE = (4, 2, 8, 2, 2)
DP = ("y", "xl", "z", "core")
PLANE = ("y", "xl")
LINE = ("z", "core")
NY, NX, NZ = 4, 2, 8
LINE_ROWS = 12


def call(kernel, outs, *args, scratch=(), after=(), final=False):
    count = len(args)

    def body(*refs):
        kernel(*refs[:count], *refs[count + len(after) :])

    return pl.pallas_call(
        body,
        out_shape=[jax.ShapeDtypeStruct(s, t) if final else pltpu.VMEM(s, t) for s, t in outs],
        in_specs=[pl.BlockSpec(memory_space=pltpu.VMEM)] * count + [pl.BlockSpec(memory_space=pl.ANY)] * len(after),
        out_specs=[pl.BlockSpec(memory_space=pltpu.VMEM) for _ in outs],
        scratch_shapes=[pltpu.VMEM(s, t) for s, t in scratch],
        compiler_params=pltpu.CompilerParams(vmem_limit_bytes=12 << 20),
    )(*args, *after)


def from_plane(x, step):
    dy, dx = step
    pairs = []
    for y in range(NY):
        for xl in range(NX):
            pairs.append((((y + dy) % NY) * NX + (xl + dx) % NX, y * NX + xl))
    return lax.ppermute(x, PLANE, pairs)


def from_line(x, step, back=False):
    pairs = []
    for z in range(NZ):
        for core in range(2):
            way = step if (core == 0) != back else -step
            pairs.append((((z + way) % NZ) * 2 + core, z * 2 + core))
    return lax.ppermute(x, LINE, pairs)


def from_core(x):
    return lax.ppermute(x, "core", [(0, 1), (1, 0)])


def pack(refs, scratch):
    at, width = 0, scratch.shape[1]
    for ref in refs:
        n = ref.shape[0]
        scratch[at : at + n, :] = ref[:, :width]
        at += n


def lanes3(x, first, shape):
    lane = lax.broadcasted_iota(I32, shape, 1)
    high = x.astype(BF16).astype(F32)
    mid = (x - high).astype(BF16).astype(F32)
    low = (x - high - mid).astype(BF16).astype(F32)
    out = jnp.zeros(shape, F32)
    for i, part in enumerate((high, mid, low)):
        out = jnp.where(lane == first + i, jnp.broadcast_to(part, shape), out)
    return out


def sum_lanes(x, first):
    lane = lax.broadcasted_iota(I32, (1, 128), 1)
    return jnp.sum(jnp.where((lane >= first) & (lane < first + 3), x[:1, :].astype(F32), 0.0), axis=1, keepdims=True)


def own_kernel(q_ref, p_ref, h_ref, pos_ref, hard_ref, own_q, own_p, pos, hard, sems):
    rows, width = q_ref.shape
    moves = [
        (pos_ref, pos),
        (hard_ref, hard),
        (q_ref, own_q.at[:, :width]),
        (p_ref, own_p.at[:rows, :]),
        (h_ref, own_p.at[rows:, :]),
    ]
    copies = [pltpu.make_async_copy(src, dst, sems.at[i]) for i, (src, dst) in enumerate(moves)]
    for copy in copies:
        copy.start()
    copies[0].wait()
    copies[1].wait()
    lane = lax.broadcasted_iota(I32, (8, 128), 1)
    row = lax.broadcasted_iota(I32, (8, 128), 0)
    ids = jnp.zeros((rows, 128), F32)
    first = jnp.broadcast_to(pos[...], (8, rows))
    for shift, part in ((0, lambda v: v >> 4), (16, lambda v: v & 15)):
        for values, at in ((hard[...], lane == row + 1 + shift), (first, (lane == shift) & (row == 0))):
            ids = ids + lax.dot_general(
                part(values).astype(F32).astype(BF16),
                jnp.where(at, 1.0, 0.0).astype(BF16),
                (((0,), (0,)), ((), ())),
                preferred_element_type=F32,
            )
    own_q[:, width:] = ids.astype(BF16)
    for copy in copies[2:]:
        copy.wait()


def place_kernel(at_ref, cols_ref, rel_ref, pool_ref):
    lane = lax.broadcasted_iota(I32, (8, 128), 1)
    y = (at_ref[0] + (lane >> 5)) & (NY - 1)
    x = (at_ref[1] + (lane >> 4)) & (NX - 1)
    line = at_ref[2] * 2 + at_ref[3]
    row = lax.broadcasted_iota(I32, (8, 128), 0)
    cols_ref[...] = jnp.where(row == 0, ((y * NX + x) * (NZ * 2) + line) * 16 + (lane & 15), line).astype(F32)
    row = lax.broadcasted_iota(I32, pool_ref.shape, 0)
    y, x = (at_ref[0] + (row >> 5)) & (NY - 1), (at_ref[1] + (row >> 4)) & (NX - 1)
    pool_ref[...] = (((y * NX + x) * (NZ * 2) + line) * 16 + (row & 15)).astype(F32)
    lane = lax.broadcasted_iota(I32, (8, 128), 1)
    rel = jnp.where(at_ref[3] == 0, at_ref[2] - lane, lane - at_ref[2]) & (NZ - 1)
    rel_ref[...] = jnp.where((lane >= NZ) | ((at_ref[3] == 1) & ((rel & 3) == 0)), NZ, rel)


def pack_kernel(*refs):
    pack(refs[:-1], refs[-1])


def split_kernel(ref, *parts):
    for i, part in enumerate(parts):
        part[...] = ref[16 * i : 16 * i + 16, :]


def far_kernel(near1, near2, far):
    far[:32, :] = near1[...]
    far[32:, :] = near2[:16, :]


def id_row(ids_ref, k):
    return ids_ref[k : k + 1, :] * 16.0 + ids_ref[16 + k : 17 + k, :]


def scores_kernel(*refs):
    q_refs, p_refs, pool_ref, (s_ref, pos_ref, ids_ref, q_all, p_all, ids_all) = refs[:8], refs[8:16], refs[16], refs[17:]
    width = p_all.shape[1]
    pack(q_refs, q_all)
    for k, ref in enumerate(p_refs):
        p_all[16 * k : 16 * k + 16, :] = ref[:16, :]
        p_all[128 + 16 * k : 144 + 16 * k, :] = ref[16:, :]
    at = 0
    for ref in q_refs:
        n = ref.shape[0]
        ids_all[at : at + n, :] = ref[:, width:]
        at += n
    across = (((1,), (1,)), ((), ()))
    s_ref[:256, :] = lax.dot_general(q_all[...], p_all[:128, :], across, preferred_element_type=F32)
    ids = ids_all[...].astype(F32)
    pos_ref[...] = jnp.broadcast_to(ids[:, :1] * 16.0 + ids[:, 16:17], pos_ref.shape)
    lane, row = lax.broadcasted_iota(I32, (128, 128), 1), lax.broadcasted_iota(I32, (128, 128), 0)
    turn = jnp.where(lane == row, 1.0, 0.0).astype(BF16)
    ids_ref[...] = lax.dot_general(turn, ids_all[...], across, preferred_element_type=F32)[:32, :]
    hard = lax.dot_general(p_all[128:, :], q_all[...], across, preferred_element_type=F32)
    for k in range(8):
        mine = jnp.where(pool_ref[...] == id_row(ids_ref, k + 1), hard, 0.0)
        picked = jnp.sum(mine, axis=0, keepdims=True)
        s_ref[256 + k : 257 + k, :] = picked[:, :128]
        s_ref[264 + k : 265 + k, :] = picked[:, 128:]


def sigmoid_softplus(logits):
    e = jnp.exp(-jnp.abs(logits))
    return jnp.where(logits >= 0.0, 1.0, e) / (1.0 + e), jnp.maximum(logits, 0.0) + jnp.log1p(e)


def sum_all(x):
    return jnp.sum(jnp.sum(x, axis=1, keepdims=True), axis=0, keepdims=True)


def weights_kernel(s_ref, got_ref, pos_ref, ids_ref, cols_ref, pool_ref, w_ref, loss_ref):
    logits = SCALE * (s_ref[...] + got_ref[...]) + LOGIT_BIAS
    sigmoid, softplus = sigmoid_softplus(logits)
    labels = (pos_ref[...] == cols_ref[:1, :]).astype(F32)
    w_ref[:, :128] = ((sigmoid[:256, :] - labels) * SCALE).astype(BF16)
    loss = sum_all(softplus[:256, :] - labels * logits[:256, :])

    line = cols_ref[1:2, :1].astype(I32)
    here = (ids_ref[1:9, :].astype(I32) & 15) == line
    hard, cost = (jnp.concatenate([x[256:264, :], x[264:, :]], axis=1) for x in (sigmoid, softplus))
    loss = loss + sum_all(jnp.where(here, cost, 0.0))
    loss_ref[...] = jnp.broadcast_to(loss, loss_ref.shape)
    hard = (hard * SCALE).astype(BF16).astype(F32)
    total = jnp.zeros(pool_ref.shape, F32)
    for k in range(8):
        total = total + jnp.where(pool_ref[...] == id_row(ids_ref, k + 1), hard[k : k + 1, :], 0.0)
    w_ref[:, 128:] = total.T.astype(BF16)


def grad_q_kernel(w_ref, p_all, loss_ref, keep_ref, send_ref):
    part = jnp.dot(w_ref[...], p_all[...], preferred_element_type=F32)
    keep_ref[...] = part[:144, :]
    send_ref[:112, :] = part[144:, :].astype(BF16)
    send_ref[112:, :128] = lanes3(loss_ref[:1, :1], 0, (16, 128)).astype(BF16)
    send_ref[112:, 128:] = jnp.zeros((16, send_ref.shape[1] - 128), BF16)


def grad_p_kernel(w_ref, q_all, own_ref, up_ref, down_ref, opposite_ref, other_ref):
    part = lax.dot_general(w_ref[...], q_all[...], (((0,), (0,)), ((), ())), preferred_element_type=F32)
    places = [(own_ref, 0), (own_ref, 32), (up_ref, 0), (up_ref, 32), (opposite_ref, 0), (other_ref, 0), (down_ref, 0)]
    for k, (ref, at) in enumerate(places + [(down_ref, 32)]):
        ref[at : at + 16, :] = part[16 * k : 16 * k + 16, :].astype(ref.dtype)
        ref[at + 16 : at + 32, :] = part[128 + 16 * k : 144 + 16 * k, :].astype(ref.dtype)


def opposite_kernel(mine_ref, got_ref, out_ref):
    out_ref[...] = (mine_ref[...] + got_ref[...].astype(F32)).astype(BF16)


def far_sum_kernel(keep_ref, got_ref, loss_ref, far_ref, chip_loss_ref):
    width = keep_ref.shape[1]
    loss = loss_ref[:1, :1] + sum_lanes(got_ref[112:, :128], 0)
    chip_loss_ref[...] = jnp.broadcast_to(loss, chip_loss_ref.shape)
    far_ref[:, :width] = (keep_ref[96:144, :] + got_ref[64:112, :].astype(F32)).astype(BF16)
    far_ref[:, width:] = lanes3(loss, 0, (48, 128)).astype(BF16)


def near_sum_kernel(keep_ref, got_ref, far_ref, loss_ref, near1_ref, near2_ref):
    width = keep_ref.shape[1]
    far_loss = sum_lanes(far_ref[:16, width:], 0)
    lanes = (lanes3(loss_ref[:1, :1], 0, (32, 128)) + lanes3(far_loss, 3, (32, 128))).astype(BF16)
    near1_ref[:, width:] = lanes
    near2_ref[:, width:] = lanes
    near1 = keep_ref[32:64, :] + got_ref[:32, :].astype(F32) + far_ref[:32, :width].astype(F32)
    near1_ref[:, :width] = near1.astype(BF16)
    near2 = keep_ref[64:80, :] + got_ref[32:48, :].astype(F32) + far_ref[32:, :width].astype(F32)
    near2_ref[:16, :width] = near2.astype(BF16)
    near2_ref[16:, :width] = (keep_ref[80:96, :] + got_ref[48:64, :].astype(F32)).astype(BF16)


def line_kernel(b1, b2, loss_ref, rel_ref, line_ref):
    width = b1.shape[1] - 128
    rel = rel_ref[:1, :]
    line = jnp.where(rel == 0, loss_ref[:1, :1], 0.0)
    for step, ref, first in ((1, b1, 0), (3, b1, 3), (2, b2, 0), (4, b2, 3)):
        line = jnp.where(rel == step, sum_lanes(ref[:16, width:], first), line)
    line_ref[...] = jnp.broadcast_to(line[None], line_ref.shape)


def chip_sum_kernel(keep_ref, b1, b2, mine_ref, theirs_ref):
    rows, width = mine_ref.shape
    total = keep_ref[: 2 * rows, :] + b1[:, :width].astype(F32) + b2[:, :width].astype(F32)
    mine_ref[...] = total[:rows, :]
    theirs_ref[...] = total[rows:, :].astype(BF16)


def row_sum_kernel(own_ref, up, down, opposite, mine_ref, theirs_ref):
    total = own_ref[...] + up[...].astype(F32) + down[...].astype(F32)
    mine_ref[...] = total[:32, :] + opposite[...].astype(F32)
    theirs_ref[...] = total[32:, :].astype(BF16)


def finish_kernel(count):
    def kernel(mine_q, got_q, mine_p, got_p, line_ref, q_ref, p_ref, h_ref, loss_ref):
        rows = q_ref.shape[0]
        q_ref[...] = (mine_q[...] + got_q[...].astype(F32)).astype(BF16)
        total = mine_p[...] + got_p[...].astype(F32)
        p_ref[...] = total[:rows, :].astype(BF16)
        h_ref[...] = total[rows:, :].astype(BF16)
        line = jnp.sum(line_ref[...], axis=0)[:1, :]
        loss_ref[...] = jnp.sum(line, axis=1, keepdims=True) / count

    return kernel


def on_device(queries, passages, hard_passages, positive_ids, hard_ids):
    rows, width = queries.shape
    wide = width + 128
    batch = rows * NY * NX * NZ * 2
    per_query = hard_ids.shape[1]

    own_q, own_p = pl.pallas_call(
        own_kernel,
        out_shape=[pltpu.VMEM((rows, wide), BF16), pltpu.VMEM((2 * rows, width), BF16)],
        in_specs=[pl.BlockSpec(memory_space=pltpu.HBM)] * 5,
        out_specs=[pl.BlockSpec(memory_space=pltpu.VMEM)] * 2,
        scratch_shapes=[pltpu.VMEM((1, rows), I32), pltpu.VMEM((per_query, rows), I32), pltpu.SemaphoreType.DMA((5,))],
        compiler_params=pltpu.CompilerParams(vmem_limit_bytes=12 << 20),
    )(
        *(
            pltpu.with_memory_space_constraint(x, pltpu.HBM)
            for x in (queries, passages, hard_passages, positive_ids.reshape(1, rows), hard_ids.T)
        )
    )
    cols, rel, pool = pl.pallas_call(
        place_kernel,
        out_shape=[pltpu.VMEM((8, 128), F32), pltpu.VMEM((8, 128), I32), pltpu.VMEM((128, 256), F32)],
        in_specs=[pl.BlockSpec(memory_space=pltpu.SMEM)],
        out_specs=[pl.BlockSpec(memory_space=pltpu.VMEM)] * 3,
    )(jnp.stack([lax.axis_index(name) for name in DP]))
    other_p = from_plane(own_p, (0, 1))
    (chip_q,) = call(pack_kernel, [((2 * rows, wide), BF16)], own_q, from_core(own_q))
    own_up, own_down = from_plane(own_p, (1, 0)), from_plane(own_p, (3, 0))
    other_up, other_down = from_plane(other_p, (1, 0)), from_plane(other_p, (3, 0))
    own_opposite = from_plane(own_p, (2, 0))
    other_opposite = from_plane(own_opposite, (0, 1))
    block_p = [own_p, other_p, own_up, other_up, own_opposite, other_opposite, own_down, other_down]
    near1, near2 = from_line(chip_q, 1), from_line(chip_q, 2)
    (far,) = call(far_kernel, [((48, wide), BF16)], near1, near2, after=[other_p])
    (both,) = call(pack_kernel, [((64, wide), BF16)], near1, near2, after=[cols, own_opposite, own_up, own_down])
    far = from_line(far, 2)
    far_parts = [from_core(x) for x in call(split_kernel, [((16, wide), BF16)] * 3, far)]

    scores, pos, ids, q_all, p_all = call(
        scores_kernel,
        [
            ((272, 128), F32),
            ((256, 128), F32),
            ((32, 256), F32),
            ((256, width), BF16),
            ((256, width), BF16),
        ],
        chip_q,
        near1,
        near2,
        far,
        from_core(both),
        *far_parts,
        *block_p,
        pool,
        scratch=[((256, 128), BF16)],
    )
    other = lax.ppermute(scores, "pair", [(0, 1), (1, 0)])
    weights, loss = call(
        weights_kernel,
        [((256, 256), BF16), ((8, 128), F32)],
        scores,
        other,
        pos,
        ids,
        cols,
        pool,
    )
    keep, send = call(
        grad_q_kernel, [((144, width), F32), ((128, width), BF16)], weights, p_all, loss
    )
    got = from_core(send)
    own, up, down, opposite, other = call(
        grad_p_kernel,
        [((64, width), F32), ((64, width), BF16), ((64, width), BF16), ((32, width), F32), ((32, width), BF16)],
        weights,
        q_all,
    )
    far, loss = call(far_sum_kernel, [((48, wide), BF16), ((8, 128), F32)], keep, got, loss, after=[own])
    (opposite,) = call(opposite_kernel, [((32, width), BF16)], opposite, from_plane(other, (0, 1)))
    parts = [from_plane(up, (3, 0)), from_plane(down, (1, 0)), from_plane(opposite, (2, 0))]
    far = from_line(far, 2, back=True)
    near1, near2 = call(near_sum_kernel, [((32, wide), BF16)] * 2, keep, got, far, loss)
    near1, near2 = from_line(near1, 1, back=True), from_line(near2, 2, back=True)
    mine_p, theirs_p = call(row_sum_kernel, [((32, width), F32), ((32, width), BF16)], own, *parts)
    (line,) = call(line_kernel, [((NY * NX * 2, LINE_ROWS, 128), F32)], near1, near2, loss, rel)
    mine, theirs = call(chip_sum_kernel, [((rows, width), F32), ((rows, width), BF16)], keep, near1, near2)
    line = lax.all_to_all(line, ("y", "xl", "core"), 0, 0, tiled=True)
    grad_q, grad_p, grad_h, mean_loss = call(
        finish_kernel(batch * (batch + per_query)),
        [((rows, width), BF16)] * 3 + [((1, 1), F32)],
        mine,
        from_core(theirs),
        mine_p,
        from_plane(theirs_p, (0, 1)),
        line,
        final=True,
    )
    return mean_loss.reshape(1), grad_q, grad_p, grad_h


def solution(mesh):
    spec = P(DP, "pair")
    return jax.shard_map(
        on_device,
        mesh=Mesh(mesh.devices.reshape(SHAPE), DP + ("pair",)),
        in_specs=(spec, spec, spec, P(DP), P(DP, None)),
        out_specs=(P(), spec, spec, spec),
        check_vma=False,
    )
```

```python
import math

import jax
import jax.numpy as jnp
from jax import lax
from jax.experimental import pallas as pl
from jax.experimental.pallas import tpu as pltpu
from jax.sharding import Mesh, PartitionSpec as P

D = 4096
SCALE = 1.0 / math.sqrt(D)
LOGIT_BIAS = -1.0
BF16, F32, I32 = jnp.bfloat16, jnp.float32, jnp.int32

SHAPE = (4, 2, 8, 2, 2)
DP = ("y", "xl", "z", "core")
PLANE = ("y", "xl")
LINE = ("z", "core")
NY, NX, NZ = 4, 2, 8
LINE_ROWS = 12


def call(kernel, outs, *args, scratch=(), after=(), final=False):
    count = len(args)

    def body(*refs):
        kernel(*refs[:count], *refs[count + len(after) :])

    return pl.pallas_call(
        body,
        out_shape=[jax.ShapeDtypeStruct(s, t) if final else pltpu.VMEM(s, t) for s, t in outs],
        in_specs=[pl.BlockSpec(memory_space=pltpu.VMEM)] * count + [pl.BlockSpec(memory_space=pl.ANY)] * len(after),
        out_specs=[pl.BlockSpec(memory_space=pltpu.VMEM) for _ in outs],
        scratch_shapes=[pltpu.VMEM(s, t) for s, t in scratch],
        compiler_params=pltpu.CompilerParams(vmem_limit_bytes=12 << 20),
    )(*args, *after)


def from_plane(x, step):
    dy, dx = step
    pairs = []
    for y in range(NY):
        for xl in range(NX):
            pairs.append((((y + dy) % NY) * NX + (xl + dx) % NX, y * NX + xl))
    return lax.ppermute(x, PLANE, pairs)


def from_line(x, step, back=False):
    pairs = []
    for z in range(NZ):
        for core in range(2):
            way = step if (core == 0) != back else -step
            pairs.append((((z + way) % NZ) * 2 + core, z * 2 + core))
    return lax.ppermute(x, LINE, pairs)


def from_core(x):
    return lax.ppermute(x, "core", [(0, 1), (1, 0)])


def pack(refs, scratch):
    at, width = 0, scratch.shape[1]
    for ref in refs:
        n = ref.shape[0]
        scratch[at : at + n, :] = ref[:, :width]
        at += n


def lanes3(x, first, shape):
    lane = lax.broadcasted_iota(I32, shape, 1)
    high = x.astype(BF16).astype(F32)
    mid = (x - high).astype(BF16).astype(F32)
    low = (x - high - mid).astype(BF16).astype(F32)
    out = jnp.zeros(shape, F32)
    for i, part in enumerate((high, mid, low)):
        out = jnp.where(lane == first + i, jnp.broadcast_to(part, shape), out)
    return out


def sum_lanes(x, first):
    lane = lax.broadcasted_iota(I32, (1, 128), 1)
    return jnp.sum(jnp.where((lane >= first) & (lane < first + 3), x[:1, :].astype(F32), 0.0), axis=1, keepdims=True)


def own_kernel(q_ref, p_ref, h_ref, pos_ref, hard_ref, own_q, own_p, pos, hard, sems):
    rows, width = q_ref.shape
    moves = [
        (pos_ref, pos),
        (hard_ref, hard),
        (q_ref, own_q.at[:, :width]),
        (p_ref, own_p.at[:rows, :]),
        (h_ref, own_p.at[rows:, :]),
    ]
    copies = [pltpu.make_async_copy(src, dst, sems.at[i]) for i, (src, dst) in enumerate(moves)]
    for copy in copies:
        copy.start()
    copies[0].wait()
    copies[1].wait()
    lane = lax.broadcasted_iota(I32, (8, 128), 1)
    row = lax.broadcasted_iota(I32, (8, 128), 0)
    ids = jnp.zeros((rows, 128), F32)
    first = jnp.broadcast_to(pos[...], (8, rows))
    for shift, part in ((0, lambda v: v >> 4), (16, lambda v: v & 15)):
        for values, at in ((hard[...], lane == row + 1 + shift), (first, (lane == shift) & (row == 0))):
            ids = ids + lax.dot_general(
                part(values).astype(F32).astype(BF16),
                jnp.where(at, 1.0, 0.0).astype(BF16),
                (((0,), (0,)), ((), ())),
                preferred_element_type=F32,
            )
    own_q[:, width:] = ids.astype(BF16)
    for copy in copies[2:]:
        copy.wait()


def place_kernel(at_ref, cols_ref, rel_ref, pool_ref):
    lane = lax.broadcasted_iota(I32, (8, 128), 1)
    y = (at_ref[0] + (lane >> 5)) & (NY - 1)
    x = (at_ref[1] + (lane >> 4)) & (NX - 1)
    line = at_ref[2] * 2 + at_ref[3]
    row = lax.broadcasted_iota(I32, (8, 128), 0)
    cols_ref[...] = jnp.where(row == 0, ((y * NX + x) * (NZ * 2) + line) * 16 + (lane & 15), line).astype(F32)
    row = lax.broadcasted_iota(I32, pool_ref.shape, 0)
    y, x = (at_ref[0] + (row >> 5)) & (NY - 1), (at_ref[1] + (row >> 4)) & (NX - 1)
    pool_ref[...] = (((y * NX + x) * (NZ * 2) + line) * 16 + (row & 15)).astype(F32)
    lane = lax.broadcasted_iota(I32, (8, 128), 1)
    rel = jnp.where(at_ref[3] == 0, at_ref[2] - lane, lane - at_ref[2]) & (NZ - 1)
    rel_ref[...] = jnp.where((lane >= NZ) | ((at_ref[3] == 1) & ((rel & 3) == 0)), NZ, rel)


def pack_kernel(*refs):
    pack(refs[:-1], refs[-1])


def split_kernel(ref, *parts):
    for i, part in enumerate(parts):
        part[...] = ref[16 * i : 16 * i + 16, :]


def far_kernel(near1, near2, far):
    far[:32, :] = near1[...]
    far[32:, :] = near2[:16, :]


def id_row(ids_ref, k):
    return ids_ref[k : k + 1, :] * 16.0 + ids_ref[16 + k : 17 + k, :]


def scores_kernel(*refs):
    q_refs, p_refs, pool_ref, (s_ref, pos_ref, ids_ref, q_all, p_all, ids_all) = refs[:8], refs[8:16], refs[16], refs[17:]
    width = p_all.shape[1]
    pack(q_refs, q_all)
    for k, ref in enumerate(p_refs):
        p_all[16 * k : 16 * k + 16, :] = ref[:16, :]
        p_all[128 + 16 * k : 144 + 16 * k, :] = ref[16:, :]
    at = 0
    for ref in q_refs:
        n = ref.shape[0]
        ids_all[at : at + n, :] = ref[:, width:]
        at += n
    across = (((1,), (1,)), ((), ()))
    s_ref[:256, :] = lax.dot_general(q_all[...], p_all[:128, :], across, preferred_element_type=F32)
    ids = ids_all[...].astype(F32)
    pos_ref[...] = jnp.broadcast_to(ids[:, :1] * 16.0 + ids[:, 16:17], pos_ref.shape)
    lane, row = lax.broadcasted_iota(I32, (128, 128), 1), lax.broadcasted_iota(I32, (128, 128), 0)
    turn = jnp.where(lane == row, 1.0, 0.0).astype(BF16)
    ids_ref[...] = lax.dot_general(turn, ids_all[...], across, preferred_element_type=F32)[:32, :]
    hard = lax.dot_general(p_all[128:, :], q_all[...], across, preferred_element_type=F32)
    for k in range(8):
        mine = jnp.where(pool_ref[...] == id_row(ids_ref, k + 1), hard, 0.0)
        picked = jnp.sum(mine, axis=0, keepdims=True)
        s_ref[256 + k : 257 + k, :] = picked[:, :128]
        s_ref[264 + k : 265 + k, :] = picked[:, 128:]


def sigmoid_softplus(logits):
    e = jnp.exp(-jnp.abs(logits))
    return jnp.where(logits >= 0.0, 1.0, e) / (1.0 + e), jnp.maximum(logits, 0.0) + jnp.log1p(e)


def sum_all(x):
    return jnp.sum(jnp.sum(x, axis=1, keepdims=True), axis=0, keepdims=True)


def weights_kernel(s_ref, got_ref, pos_ref, ids_ref, cols_ref, pool_ref, w_ref, loss_ref):
    logits = SCALE * (s_ref[...] + got_ref[...]) + LOGIT_BIAS
    sigmoid, softplus = sigmoid_softplus(logits)
    labels = (pos_ref[...] == cols_ref[:1, :]).astype(F32)
    w_ref[:, :128] = ((sigmoid[:256, :] - labels) * SCALE).astype(BF16)
    loss = sum_all(softplus[:256, :] - labels * logits[:256, :])

    line = cols_ref[1:2, :1].astype(I32)
    here = (ids_ref[1:9, :].astype(I32) & 15) == line
    hard, cost = (jnp.concatenate([x[256:264, :], x[264:, :]], axis=1) for x in (sigmoid, softplus))
    loss = loss + sum_all(jnp.where(here, cost, 0.0))
    loss_ref[...] = jnp.broadcast_to(loss, loss_ref.shape)
    hard = (hard * SCALE).astype(BF16).astype(F32)
    total = jnp.zeros(pool_ref.shape, F32)
    for k in range(8):
        total = total + jnp.where(pool_ref[...] == id_row(ids_ref, k + 1), hard[k : k + 1, :], 0.0)
    w_ref[:, 128:] = total.T.astype(BF16)


def grad_far_kernel(w_ref, p_all, loss_ref, keep_ref, send_ref):
    rows = jnp.concatenate([w_ref[96:144, :], w_ref[208:, :]], axis=0)
    part = jnp.dot(rows, p_all[...], preferred_element_type=F32)
    keep_ref[...] = part[:48, :]
    send_ref[:48, :] = part[48:, :].astype(BF16)
    send_ref[48:, :128] = lanes3(loss_ref[:1, :1], 0, (16, 128)).astype(BF16)
    send_ref[48:, 128:] = jnp.zeros((16, send_ref.shape[1] - 128), BF16)


def grad_near_kernel(w_ref, p_all, keep_ref, send_ref):
    rows = jnp.concatenate([w_ref[:96, :], w_ref[144:208, :]], axis=0)
    part = jnp.dot(rows, p_all[...], preferred_element_type=F32)
    keep_ref[...] = part[:96, :]
    send_ref[...] = part[96:, :].astype(BF16)


def grad_p_kernel(w_ref, q_all, own_ref, up_ref, down_ref, opposite_ref, other_ref):
    part = lax.dot_general(w_ref[...], q_all[...], (((0,), (0,)), ((), ())), preferred_element_type=F32)
    places = [(own_ref, 0), (own_ref, 32), (up_ref, 0), (up_ref, 32), (opposite_ref, 0), (other_ref, 0), (down_ref, 0)]
    for k, (ref, at) in enumerate(places + [(down_ref, 32)]):
        ref[at : at + 16, :] = part[16 * k : 16 * k + 16, :].astype(ref.dtype)
        ref[at + 16 : at + 32, :] = part[128 + 16 * k : 144 + 16 * k, :].astype(ref.dtype)


def opposite_kernel(mine_ref, got_ref, out_ref):
    out_ref[...] = (mine_ref[...] + got_ref[...].astype(F32)).astype(BF16)


def far_sum_kernel(keep_ref, got_ref, loss_ref, far_ref, chip_loss_ref):
    width = keep_ref.shape[1]
    loss = loss_ref[:1, :1] + sum_lanes(got_ref[48:, :128], 0)
    chip_loss_ref[...] = jnp.broadcast_to(loss, chip_loss_ref.shape)
    far_ref[:, :width] = (keep_ref[...] + got_ref[:48, :].astype(F32)).astype(BF16)
    far_ref[:, width:] = lanes3(loss, 0, (48, 128)).astype(BF16)


def near_sum_kernel(keep_ref, got_ref, far_ref, loss_ref, near1_ref, near2_ref):
    width = keep_ref.shape[1]
    far_loss = sum_lanes(far_ref[:16, width:], 0)
    lanes = (lanes3(loss_ref[:1, :1], 0, (32, 128)) + lanes3(far_loss, 3, (32, 128))).astype(BF16)
    near1_ref[:, width:] = lanes
    near2_ref[:, width:] = lanes
    near1 = keep_ref[32:64, :] + got_ref[:32, :].astype(F32) + far_ref[:32, :width].astype(F32)
    near1_ref[:, :width] = near1.astype(BF16)
    near2 = keep_ref[64:80, :] + got_ref[32:48, :].astype(F32) + far_ref[32:, :width].astype(F32)
    near2_ref[:16, :width] = near2.astype(BF16)
    near2_ref[16:, :width] = (keep_ref[80:96, :] + got_ref[48:64, :].astype(F32)).astype(BF16)


def line_kernel(b1, b2, loss_ref, rel_ref, line_ref):
    width = b1.shape[1] - 128
    rel = rel_ref[:1, :]
    line = jnp.where(rel == 0, loss_ref[:1, :1], 0.0)
    for step, ref, first in ((1, b1, 0), (3, b1, 3), (2, b2, 0), (4, b2, 3)):
        line = jnp.where(rel == step, sum_lanes(ref[:16, width:], first), line)
    line_ref[...] = jnp.broadcast_to(line[None], line_ref.shape)


def chip_sum_kernel(keep_ref, b1, b2, mine_ref, theirs_ref):
    rows, width = mine_ref.shape
    total = keep_ref[: 2 * rows, :] + b1[:, :width].astype(F32) + b2[:, :width].astype(F32)
    mine_ref[...] = total[:rows, :]
    theirs_ref[...] = total[rows:, :].astype(BF16)


def row_sum_kernel(own_ref, up, down, opposite, mine_ref, theirs_ref):
    total = own_ref[...] + up[...].astype(F32) + down[...].astype(F32)
    mine_ref[...] = total[:32, :] + opposite[...].astype(F32)
    theirs_ref[...] = total[32:, :].astype(BF16)


def finish_kernel(count):
    def kernel(mine_q, got_q, mine_p, got_p, line_ref, q_ref, p_ref, h_ref, loss_ref):
        rows = q_ref.shape[0]
        q_ref[...] = (mine_q[...] + got_q[...].astype(F32)).astype(BF16)
        total = mine_p[...] + got_p[...].astype(F32)
        p_ref[...] = total[:rows, :].astype(BF16)
        h_ref[...] = total[rows:, :].astype(BF16)
        line = jnp.sum(line_ref[...], axis=0)[:1, :]
        loss_ref[...] = jnp.sum(line, axis=1, keepdims=True) / count

    return kernel


def on_device(queries, passages, hard_passages, positive_ids, hard_ids):
    rows, width = queries.shape
    wide = width + 128
    batch = rows * NY * NX * NZ * 2
    per_query = hard_ids.shape[1]

    own_q, own_p = pl.pallas_call(
        own_kernel,
        out_shape=[pltpu.VMEM((rows, wide), BF16), pltpu.VMEM((2 * rows, width), BF16)],
        in_specs=[pl.BlockSpec(memory_space=pltpu.HBM)] * 5,
        out_specs=[pl.BlockSpec(memory_space=pltpu.VMEM)] * 2,
        scratch_shapes=[pltpu.VMEM((1, rows), I32), pltpu.VMEM((per_query, rows), I32), pltpu.SemaphoreType.DMA((5,))],
        compiler_params=pltpu.CompilerParams(vmem_limit_bytes=12 << 20),
    )(
        *(
            pltpu.with_memory_space_constraint(x, pltpu.HBM)
            for x in (queries, passages, hard_passages, positive_ids.reshape(1, rows), hard_ids.T)
        )
    )
    cols, rel, pool = pl.pallas_call(
        place_kernel,
        out_shape=[pltpu.VMEM((8, 128), F32), pltpu.VMEM((8, 128), I32), pltpu.VMEM((128, 256), F32)],
        in_specs=[pl.BlockSpec(memory_space=pltpu.SMEM)],
        out_specs=[pl.BlockSpec(memory_space=pltpu.VMEM)] * 3,
    )(jnp.stack([lax.axis_index(name) for name in DP]))
    other_p = from_plane(own_p, (0, 1))
    (chip_q,) = call(pack_kernel, [((2 * rows, wide), BF16)], own_q, from_core(own_q))
    own_up, own_down = from_plane(own_p, (1, 0)), from_plane(own_p, (3, 0))
    other_up, other_down = from_plane(other_p, (1, 0)), from_plane(other_p, (3, 0))
    own_opposite = from_plane(own_p, (2, 0))
    other_opposite = from_plane(own_opposite, (0, 1))
    block_p = [own_p, other_p, own_up, other_up, own_opposite, other_opposite, own_down, other_down]
    near1, near2 = from_line(chip_q, 1), from_line(chip_q, 2)
    (far,) = call(far_kernel, [((48, wide), BF16)], near1, near2, after=[other_p])
    (both,) = call(pack_kernel, [((64, wide), BF16)], near1, near2, after=[cols, own_opposite, own_up, own_down])
    far = from_line(far, 2)
    far_parts = [from_core(x) for x in call(split_kernel, [((16, wide), BF16)] * 3, far)]

    scores, pos, ids, q_all, p_all = call(
        scores_kernel,
        [
            ((272, 128), F32),
            ((256, 128), F32),
            ((32, 256), F32),
            ((256, width), BF16),
            ((256, width), BF16),
        ],
        chip_q,
        near1,
        near2,
        far,
        from_core(both),
        *far_parts,
        *block_p,
        pool,
        scratch=[((256, 128), BF16)],
    )
    other = lax.ppermute(scores, "pair", [(0, 1), (1, 0)])
    weights, loss = call(
        weights_kernel,
        [((256, 256), BF16), ((8, 128), F32)],
        scores,
        other,
        pos,
        ids,
        cols,
        pool,
    )
    keep_far, send_far = call(
        grad_far_kernel, [((48, width), F32), ((64, width), BF16)], weights, p_all, loss
    )
    got_far = from_core(send_far)
    keep, send = call(
        grad_near_kernel, [((96, width), F32), ((64, width), BF16)], weights, p_all, after=[send_far]
    )
    got = from_core(send)
    own, up, down, opposite, other = call(
        grad_p_kernel,
        [((64, width), F32), ((64, width), BF16), ((64, width), BF16), ((32, width), F32), ((32, width), BF16)],
        weights,
        q_all,
    )
    far, loss = call(far_sum_kernel, [((48, wide), BF16), ((8, 128), F32)], keep_far, got_far, loss, after=[own])
    (opposite,) = call(opposite_kernel, [((32, width), BF16)], opposite, from_plane(other, (0, 1)))
    parts = [from_plane(up, (3, 0)), from_plane(down, (1, 0)), from_plane(opposite, (2, 0))]
    far = from_line(far, 2, back=True)
    near1, near2 = call(near_sum_kernel, [((32, wide), BF16)] * 2, keep, got, far, loss)
    near1, near2 = from_line(near1, 1, back=True), from_line(near2, 2, back=True)
    mine_p, theirs_p = call(row_sum_kernel, [((32, width), F32), ((32, width), BF16)], own, *parts)
    (line,) = call(line_kernel, [((NY * NX * 2, LINE_ROWS, 128), F32)], near1, near2, loss, rel)
    mine, theirs = call(chip_sum_kernel, [((rows, width), F32), ((rows, width), BF16)], keep, near1, near2)
    line = lax.all_to_all(line, ("y", "xl", "core"), 0, 0, tiled=True)
    grad_q, grad_p, grad_h, mean_loss = call(
        finish_kernel(batch * (batch + per_query)),
        [((rows, width), BF16)] * 3 + [((1, 1), F32)],
        mine,
        from_core(theirs),
        mine_p,
        from_plane(theirs_p, (0, 1)),
        line,
        final=True,
    )
    return mean_loss.reshape(1), grad_q, grad_p, grad_h


def solution(mesh):
    spec = P(DP, "pair")
    return jax.shard_map(
        on_device,
        mesh=Mesh(mesh.devices.reshape(SHAPE), DP + ("pair",)),
        in_specs=(spec, spec, spec, P(DP), P(DP, None)),
        out_specs=(P(), spec, spec, spec),
        check_vma=False,
    )
```

```python
import math

import jax
import jax.numpy as jnp
from jax import lax
from jax.experimental import pallas as pl
from jax.experimental.pallas import tpu as pltpu
from jax.sharding import Mesh, PartitionSpec as P

D = 4096
SCALE = 1.0 / math.sqrt(D)
LOGIT_BIAS = -1.0
BF16, F32, I32 = jnp.bfloat16, jnp.float32, jnp.int32

SHAPE = (4, 2, 8, 2, 2)
DP = ("y", "xl", "z", "core")
PLANE = ("y", "xl")
LINE = ("z", "core")
NY, NX, NZ = 4, 2, 8
LINE_ROWS = 12


def call(kernel, outs, *args, scratch=(), after=(), final=False):
    count = len(args)

    def body(*refs):
        kernel(*refs[:count], *refs[count + len(after) :])

    return pl.pallas_call(
        body,
        out_shape=[jax.ShapeDtypeStruct(s, t) if final else pltpu.VMEM(s, t) for s, t in outs],
        in_specs=[pl.BlockSpec(memory_space=pltpu.VMEM)] * count + [pl.BlockSpec(memory_space=pl.ANY)] * len(after),
        out_specs=[pl.BlockSpec(memory_space=pltpu.VMEM) for _ in outs],
        scratch_shapes=[pltpu.VMEM(s, t) for s, t in scratch],
        compiler_params=pltpu.CompilerParams(vmem_limit_bytes=12 << 20),
    )(*args, *after)


def from_plane(x, step):
    dy, dx = step
    pairs = []
    for y in range(NY):
        for xl in range(NX):
            pairs.append((((y + dy) % NY) * NX + (xl + dx) % NX, y * NX + xl))
    return lax.ppermute(x, PLANE, pairs)


def from_line(x, step, back=False):
    pairs = []
    for z in range(NZ):
        for core in range(2):
            way = step if (core == 0) != back else -step
            pairs.append((((z + way) % NZ) * 2 + core, z * 2 + core))
    return lax.ppermute(x, LINE, pairs)


def from_core(x):
    return lax.ppermute(x, "core", [(0, 1), (1, 0)])


def pack(refs, scratch):
    at, width = 0, scratch.shape[1]
    for ref in refs:
        n = ref.shape[0]
        scratch[at : at + n, :] = ref[:, :width]
        at += n


def lanes3(x, first, shape):
    lane = lax.broadcasted_iota(I32, shape, 1)
    high = x.astype(BF16).astype(F32)
    mid = (x - high).astype(BF16).astype(F32)
    low = (x - high - mid).astype(BF16).astype(F32)
    out = jnp.zeros(shape, F32)
    for i, part in enumerate((high, mid, low)):
        out = jnp.where(lane == first + i, jnp.broadcast_to(part, shape), out)
    return out


def sum_lanes(x, first):
    lane = lax.broadcasted_iota(I32, (1, 128), 1)
    return jnp.sum(jnp.where((lane >= first) & (lane < first + 3), x[:1, :].astype(F32), 0.0), axis=1, keepdims=True)


def own_kernel(q_ref, p_ref, h_ref, pos_ref, hard_ref, own_q, own_p, pos, hard, sems):
    rows, width = q_ref.shape
    moves = [
        (pos_ref, pos),
        (hard_ref, hard),
        (q_ref, own_q.at[:, :width]),
        (p_ref, own_p.at[:rows, :]),
        (h_ref, own_p.at[rows:, :]),
    ]
    copies = [pltpu.make_async_copy(src, dst, sems.at[i]) for i, (src, dst) in enumerate(moves)]
    for copy in copies:
        copy.start()
    copies[0].wait()
    copies[1].wait()
    lane = lax.broadcasted_iota(I32, (8, 128), 1)
    row = lax.broadcasted_iota(I32, (8, 128), 0)
    ids = jnp.zeros((rows, 128), F32)
    first = jnp.broadcast_to(pos[...], (8, rows))
    for shift, part in ((0, lambda v: v >> 4), (16, lambda v: v & 15)):
        for values, at in ((hard[...], lane == row + 1 + shift), (first, (lane == shift) & (row == 0))):
            ids = ids + lax.dot_general(
                part(values).astype(F32).astype(BF16),
                jnp.where(at, 1.0, 0.0).astype(BF16),
                (((0,), (0,)), ((), ())),
                preferred_element_type=F32,
            )
    own_q[:, width:] = ids.astype(BF16)
    for copy in copies[2:]:
        copy.wait()


def place_kernel(at_ref, cols_ref, rel_ref, pool_ref):
    lane = lax.broadcasted_iota(I32, (8, 128), 1)
    y = (at_ref[0] + (lane >> 5)) & (NY - 1)
    x = (at_ref[1] + (lane >> 4)) & (NX - 1)
    line = at_ref[2] * 2 + at_ref[3]
    row = lax.broadcasted_iota(I32, (8, 128), 0)
    cols_ref[...] = jnp.where(row == 0, ((y * NX + x) * (NZ * 2) + line) * 16 + (lane & 15), line).astype(F32)
    row = lax.broadcasted_iota(I32, pool_ref.shape, 0)
    y, x = (at_ref[0] + (row >> 5)) & (NY - 1), (at_ref[1] + (row >> 4)) & (NX - 1)
    pool_ref[...] = (((y * NX + x) * (NZ * 2) + line) * 16 + (row & 15)).astype(F32)
    lane = lax.broadcasted_iota(I32, (8, 128), 1)
    rel = jnp.where(at_ref[3] == 0, at_ref[2] - lane, lane - at_ref[2]) & (NZ - 1)
    rel_ref[...] = jnp.where((lane >= NZ) | ((at_ref[3] == 1) & ((rel & 3) == 0)), NZ, rel)


def pack_kernel(*refs):
    pack(refs[:-1], refs[-1])


def split_kernel(ref, *parts):
    for i, part in enumerate(parts):
        part[...] = ref[16 * i : 16 * i + 16, :]


def far_kernel(near1, near2, far):
    far[:32, :] = near1[...]
    far[32:, :] = near2[:16, :]


def id_row(ids_ref, k):
    return ids_ref[k : k + 1, :] * 16.0 + ids_ref[16 + k : 17 + k, :]


def scores_kernel(*refs):
    q_refs, p_refs, pool_ref, (s_ref, pos_ref, ids_ref, q_all, p_all, ids_all) = refs[:8], refs[8:16], refs[16], refs[17:]
    width = p_all.shape[1]
    pack(q_refs, q_all)
    for k, ref in enumerate(p_refs):
        p_all[16 * k : 16 * k + 16, :] = ref[:16, :]
        p_all[128 + 16 * k : 144 + 16 * k, :] = ref[16:, :]
    at = 0
    for ref in q_refs:
        n = ref.shape[0]
        ids_all[at : at + n, :] = ref[:, width:]
        at += n
    across = (((1,), (1,)), ((), ()))
    s_ref[:256, :] = lax.dot_general(q_all[...], p_all[:128, :], across, preferred_element_type=F32)
    ids = ids_all[...].astype(F32)
    pos_ref[...] = jnp.broadcast_to(ids[:, :1] * 16.0 + ids[:, 16:17], pos_ref.shape)
    lane, row = lax.broadcasted_iota(I32, (128, 128), 1), lax.broadcasted_iota(I32, (128, 128), 0)
    turn = jnp.where(lane == row, 1.0, 0.0).astype(BF16)
    ids_ref[...] = lax.dot_general(turn, ids_all[...], across, preferred_element_type=F32)[:32, :]
    hard = lax.dot_general(p_all[128:, :], q_all[...], across, preferred_element_type=F32)
    for k in range(8):
        mine = jnp.where(pool_ref[...] == id_row(ids_ref, k + 1), hard, 0.0)
        picked = jnp.sum(mine, axis=0, keepdims=True)
        s_ref[256 + k : 257 + k, :] = picked[:, :128]
        s_ref[264 + k : 265 + k, :] = picked[:, 128:]


def sigmoid_softplus(logits):
    e = jnp.exp(-jnp.abs(logits))
    return jnp.where(logits >= 0.0, 1.0, e) / (1.0 + e), jnp.maximum(logits, 0.0) + jnp.log1p(e)


def sum_all(x):
    return jnp.sum(jnp.sum(x, axis=1, keepdims=True), axis=0, keepdims=True)


def weights_kernel(s_ref, got_ref, pos_ref, ids_ref, cols_ref, pool_ref, p_all, w_ref, loss_ref, keep_ref, send_ref):
    logits = SCALE * (s_ref[...] + got_ref[...]) + LOGIT_BIAS
    sigmoid, softplus = sigmoid_softplus(logits)
    labels = (pos_ref[...] == cols_ref[:1, :]).astype(F32)
    w_ref[:, :128] = ((sigmoid[:256, :] - labels) * SCALE).astype(BF16)
    loss = sum_all(softplus[:256, :] - labels * logits[:256, :])

    line = cols_ref[1:2, :1].astype(I32)
    here = (ids_ref[1:9, :].astype(I32) & 15) == line
    hard, cost = (jnp.concatenate([x[256:264, :], x[264:, :]], axis=1) for x in (sigmoid, softplus))
    loss = loss + sum_all(jnp.where(here, cost, 0.0))
    loss_ref[...] = jnp.broadcast_to(loss, loss_ref.shape)
    hard = (hard * SCALE).astype(BF16).astype(F32)
    total = jnp.zeros(pool_ref.shape, F32)
    for k in range(8):
        total = total + jnp.where(pool_ref[...] == id_row(ids_ref, k + 1), hard[k : k + 1, :], 0.0)
    w_ref[:, 128:] = total.T.astype(BF16)

    rows = jnp.concatenate([w_ref[96:144, :], w_ref[208:, :]], axis=0)
    part = jnp.dot(rows, p_all[...], preferred_element_type=F32)
    keep_ref[...] = part[:48, :]
    send_ref[:48, :] = part[48:, :].astype(BF16)
    send_ref[48:, :128] = lanes3(loss, 0, (16, 128)).astype(BF16)
    send_ref[48:, 128:] = jnp.zeros((16, send_ref.shape[1] - 128), BF16)


def grad_near_kernel(w_ref, p_all, keep_ref, send_ref):
    rows = jnp.concatenate([w_ref[:96, :], w_ref[144:208, :]], axis=0)
    part = jnp.dot(rows, p_all[...], preferred_element_type=F32)
    keep_ref[...] = part[:96, :]
    send_ref[...] = part[96:, :].astype(BF16)


def grad_p_kernel(w_ref, q_all, own_ref, up_ref, down_ref, opposite_ref, other_ref):
    part = lax.dot_general(w_ref[...], q_all[...], (((0,), (0,)), ((), ())), preferred_element_type=F32)
    places = [(own_ref, 0), (own_ref, 32), (up_ref, 0), (up_ref, 32), (opposite_ref, 0), (other_ref, 0), (down_ref, 0)]
    for k, (ref, at) in enumerate(places + [(down_ref, 32)]):
        ref[at : at + 16, :] = part[16 * k : 16 * k + 16, :].astype(ref.dtype)
        ref[at + 16 : at + 32, :] = part[128 + 16 * k : 144 + 16 * k, :].astype(ref.dtype)


def opposite_kernel(mine_ref, got_ref, out_ref):
    out_ref[...] = (mine_ref[...] + got_ref[...].astype(F32)).astype(BF16)


def far_sum_kernel(keep_ref, got_ref, loss_ref, far_ref, chip_loss_ref):
    width = keep_ref.shape[1]
    loss = loss_ref[:1, :1] + sum_lanes(got_ref[48:, :128], 0)
    chip_loss_ref[...] = jnp.broadcast_to(loss, chip_loss_ref.shape)
    far_ref[:, :width] = (keep_ref[...] + got_ref[:48, :].astype(F32)).astype(BF16)
    far_ref[:, width:] = lanes3(loss, 0, (48, 128)).astype(BF16)


def near_sum_kernel(keep_ref, got_ref, far_ref, loss_ref, near1_ref, near2_ref):
    width = keep_ref.shape[1]
    far_loss = sum_lanes(far_ref[:16, width:], 0)
    lanes = (lanes3(loss_ref[:1, :1], 0, (32, 128)) + lanes3(far_loss, 3, (32, 128))).astype(BF16)
    near1_ref[:, width:] = lanes
    near2_ref[:, width:] = lanes
    near1 = keep_ref[32:64, :] + got_ref[:32, :].astype(F32) + far_ref[:32, :width].astype(F32)
    near1_ref[:, :width] = near1.astype(BF16)
    near2 = keep_ref[64:80, :] + got_ref[32:48, :].astype(F32) + far_ref[32:, :width].astype(F32)
    near2_ref[:16, :width] = near2.astype(BF16)
    near2_ref[16:, :width] = (keep_ref[80:96, :] + got_ref[48:64, :].astype(F32)).astype(BF16)


def line_kernel(b1, b2, loss_ref, rel_ref, line_ref):
    width = b1.shape[1] - 128
    rel = rel_ref[:1, :]
    line = jnp.where(rel == 0, loss_ref[:1, :1], 0.0)
    for step, ref, first in ((1, b1, 0), (3, b1, 3), (2, b2, 0), (4, b2, 3)):
        line = jnp.where(rel == step, sum_lanes(ref[:16, width:], first), line)
    line_ref[...] = jnp.broadcast_to(line[None], line_ref.shape)


def chip_sum_kernel(keep_ref, b1, b2, mine_ref, theirs_ref):
    rows, width = mine_ref.shape
    total = keep_ref[: 2 * rows, :] + b1[:, :width].astype(F32) + b2[:, :width].astype(F32)
    mine_ref[...] = total[:rows, :]
    theirs_ref[...] = total[rows:, :].astype(BF16)


def row_sum_kernel(own_ref, up, down, opposite, mine_ref, theirs_ref):
    total = own_ref[...] + up[...].astype(F32) + down[...].astype(F32)
    mine_ref[...] = total[:32, :] + opposite[...].astype(F32)
    theirs_ref[...] = total[32:, :].astype(BF16)


def finish_kernel(count):
    def kernel(mine_q, got_q, mine_p, got_p, line_ref, q_ref, p_ref, h_ref, loss_ref):
        rows = q_ref.shape[0]
        q_ref[...] = (mine_q[...] + got_q[...].astype(F32)).astype(BF16)
        total = mine_p[...] + got_p[...].astype(F32)
        p_ref[...] = total[:rows, :].astype(BF16)
        h_ref[...] = total[rows:, :].astype(BF16)
        line = jnp.sum(line_ref[...], axis=0)[:1, :]
        loss_ref[...] = jnp.sum(line, axis=1, keepdims=True) / count

    return kernel


def on_device(queries, passages, hard_passages, positive_ids, hard_ids):
    rows, width = queries.shape
    wide = width + 128
    batch = rows * NY * NX * NZ * 2
    per_query = hard_ids.shape[1]

    own_q, own_p = pl.pallas_call(
        own_kernel,
        out_shape=[pltpu.VMEM((rows, wide), BF16), pltpu.VMEM((2 * rows, width), BF16)],
        in_specs=[pl.BlockSpec(memory_space=pltpu.HBM)] * 5,
        out_specs=[pl.BlockSpec(memory_space=pltpu.VMEM)] * 2,
        scratch_shapes=[pltpu.VMEM((1, rows), I32), pltpu.VMEM((per_query, rows), I32), pltpu.SemaphoreType.DMA((5,))],
        compiler_params=pltpu.CompilerParams(vmem_limit_bytes=12 << 20),
    )(
        *(
            pltpu.with_memory_space_constraint(x, pltpu.HBM)
            for x in (queries, passages, hard_passages, positive_ids.reshape(1, rows), hard_ids.T)
        )
    )
    cols, rel, pool = pl.pallas_call(
        place_kernel,
        out_shape=[pltpu.VMEM((8, 128), F32), pltpu.VMEM((8, 128), I32), pltpu.VMEM((128, 256), F32)],
        in_specs=[pl.BlockSpec(memory_space=pltpu.SMEM)],
        out_specs=[pl.BlockSpec(memory_space=pltpu.VMEM)] * 3,
    )(jnp.stack([lax.axis_index(name) for name in DP]))
    other_p = from_plane(own_p, (0, 1))
    (chip_q,) = call(pack_kernel, [((2 * rows, wide), BF16)], own_q, from_core(own_q))
    own_up, own_down = from_plane(own_p, (1, 0)), from_plane(own_p, (3, 0))
    other_up, other_down = from_plane(other_p, (1, 0)), from_plane(other_p, (3, 0))
    own_opposite = from_plane(own_p, (2, 0))
    other_opposite = from_plane(own_opposite, (0, 1))
    block_p = [own_p, other_p, own_up, other_up, own_opposite, other_opposite, own_down, other_down]
    near1, near2 = from_line(chip_q, 1), from_line(chip_q, 2)
    (far,) = call(far_kernel, [((48, wide), BF16)], near1, near2, after=[other_p])
    (both,) = call(pack_kernel, [((64, wide), BF16)], near1, near2, after=[cols, own_opposite, own_up, own_down])
    far = from_line(far, 2)
    far_parts = [from_core(x) for x in call(split_kernel, [((16, wide), BF16)] * 3, far)]

    scores, pos, ids, q_all, p_all = call(
        scores_kernel,
        [
            ((272, 128), F32),
            ((256, 128), F32),
            ((32, 256), F32),
            ((256, width), BF16),
            ((256, width), BF16),
        ],
        chip_q,
        near1,
        near2,
        far,
        from_core(both),
        *far_parts,
        *block_p,
        pool,
        scratch=[((256, 128), BF16)],
    )
    other = lax.ppermute(scores, "pair", [(0, 1), (1, 0)])
    weights, loss, keep_far, send_far = call(
        weights_kernel,
        [((256, 256), BF16), ((8, 128), F32), ((48, width), F32), ((64, width), BF16)],
        scores,
        other,
        pos,
        ids,
        cols,
        pool,
        p_all,
    )
    got_far = from_core(send_far)
    keep, send = call(
        grad_near_kernel, [((96, width), F32), ((64, width), BF16)], weights, p_all, after=[send_far]
    )
    got = from_core(send)
    own, up, down, opposite, other = call(
        grad_p_kernel,
        [((64, width), F32), ((64, width), BF16), ((64, width), BF16), ((32, width), F32), ((32, width), BF16)],
        weights,
        q_all,
    )
    far, loss = call(far_sum_kernel, [((48, wide), BF16), ((8, 128), F32)], keep_far, got_far, loss, after=[own])
    (opposite,) = call(opposite_kernel, [((32, width), BF16)], opposite, from_plane(other, (0, 1)))
    parts = [from_plane(up, (3, 0)), from_plane(down, (1, 0)), from_plane(opposite, (2, 0))]
    far = from_line(far, 2, back=True)
    near1, near2 = call(near_sum_kernel, [((32, wide), BF16)] * 2, keep, got, far, loss)
    near1, near2 = from_line(near1, 1, back=True), from_line(near2, 2, back=True)
    mine_p, theirs_p = call(row_sum_kernel, [((32, width), F32), ((32, width), BF16)], own, *parts)
    (line,) = call(line_kernel, [((NY * NX * 2, LINE_ROWS, 128), F32)], near1, near2, loss, rel)
    mine, theirs = call(chip_sum_kernel, [((rows, width), F32), ((rows, width), BF16)], keep, near1, near2)
    line = lax.all_to_all(line, ("y", "xl", "core"), 0, 0, tiled=True)
    grad_q, grad_p, grad_h, mean_loss = call(
        finish_kernel(batch * (batch + per_query)),
        [((rows, width), BF16)] * 3 + [((1, 1), F32)],
        mine,
        from_core(theirs),
        mine_p,
        from_plane(theirs_p, (0, 1)),
        line,
        final=True,
    )
    return mean_loss.reshape(1), grad_q, grad_p, grad_h


def solution(mesh):
    spec = P(DP, "pair")
    return jax.shard_map(
        on_device,
        mesh=Mesh(mesh.devices.reshape(SHAPE), DP + ("pair",)),
        in_specs=(spec, spec, spec, P(DP), P(DP, None)),
        out_specs=(P(), spec, spec, spec),
        check_vma=False,
    )
```
